128 devices in a mesh: dp: 32 (over x, z, core), sub: 4 (over y).
Axes of the slice: x: 4, y: 4, z: 4, core: 2. Of those that a mesh axis runs over, the one named last changes fastest.
Arguments:
- vector_window: bfloat16 [131072, 1024], P(('dp', 'sub')), may hold values from -6 to 6
- orthogonal_matrix: bfloat16 [1024, 1024], replicated, may hold values from -0.1875 to 0.1875
- centroid_table: bfloat16 [4, 2048, 256], P('sub', 'dp'), may hold values from -3.4 to 3.4
- sharpness_scale: float32 [4], replicated, may hold values from 0.25 to 1
Outputs:
- new_codebook: float32 [4, 2048, 256], P('sub', 'dp')
- recon: bfloat16 [131072, 1024], P(('dp', 'sub'))
- cross_cov: float32 [1024, 1024], replicated
The draws below stay inside these ranges and needn't reach their ends.
All inputs are finite; a program needn't handle non-finite values.
Results may differ from the reference program's by a relative error of at most 0.014.
Values may be sent and summed in bfloat16 or wider, within the bound.
A program may use at most 128 MiB of HBM per device.

```python
import math
import jax
import jax.numpy as jnp
from jax import lax

PART_TOTAL = 4
PART_FEATURES = 256
K = 2048
D = 1024
ROWS = 131072


def draw_centroid_table(key, part):
    key = jax.random.fold_in(key, 11)
    first, second = jax.random.split(key)
    values = jnp.clip(jax.random.normal(first, (PART_TOTAL, K, PART_FEATURES), jnp.float32), -4.0, 4.0)
    scales = jnp.exp(jax.random.uniform(second, (PART_TOTAL, K, 1), jnp.float32, math.log(0.7), math.log(1.4)))
    result = 0.25 * values * scales
    return result.astype(jnp.bfloat16)


def block_levels(key, shape, cuts, low, top_value):
    loudness, own = 1.0, jax.random.fold_in(key, 6)
    for position, blocks in cuts:
        draws = jnp.exp(jax.random.uniform(jax.random.fold_in(own, position), (blocks,), jnp.float32, low / len(cuts), top_value / len(cuts)))
        loudness = loudness * jnp.repeat(draws, shape[position] // blocks).reshape([-1 if axis == position else 1 for axis in range(len(shape))])
    return loudness


def normal_values(own_key, dims, scale, bound, shards=(), held_as=jnp.bfloat16):
    entries = scale * jax.random.normal(own_key, dims, jnp.float32)
    if shards:
        entries = entries * block_levels(own_key, dims, shards, -0.22, 0.18)
    return jnp.clip(entries, -bound, bound).astype(held_as)


def setup_inputs(seed: int = 0) -> dict:
    arg_keys = jax.random.split(jax.random.key(seed), 5)
    vector_window = normal_values(arg_keys[0], (ROWS, D), 1.0, 6.0, ((0, 128),))
    orthogonal_matrix = normal_values(arg_keys[1], (D, D), D ** -0.5, 0.1875)
    centroid_table = draw_centroid_table(jax.random.fold_in(arg_keys[4], 71), 0)
    sharpness_scale = jnp.clip(jnp.exp(jax.random.uniform(arg_keys[3], (PART_TOTAL,), jnp.float32, math.log(0.25), math.log(1.0))), 0.25, 1.0)
    return dict(vector_window=vector_window, orthogonal_matrix=orthogonal_matrix, centroid_table=centroid_table, sharpness_scale=sharpness_scale)


def allot_part_vectors(sample_vectors, centroid_entry, sharpness_factor):
    block = min(2048, ROWS)
    blocks = sample_vectors.reshape(ROWS // block, block, PART_FEATURES)
    centroid_norm_squared = lax.optimization_barrier(jnp.sum(centroid_entry.astype(jnp.float32) ** 2, axis=1))

    def step(carry, block_index):
        centroid_totals, centroid_tallies = carry
        raw_scores = sharpness_factor * (2.0 * jnp.dot(block_index, centroid_entry.T, preferred_element_type=jnp.float32) - centroid_norm_squared[None, :])
        probs = jax.nn.softmax(raw_scores, axis=1).astype(jnp.bfloat16)
        restored_vectors = jnp.dot(probs, centroid_entry, preferred_element_type=jnp.float32).astype(jnp.bfloat16)
        centroid_totals = centroid_totals + lax.dot_general(probs, block_index, (((0,), (0,)), ((), ())), preferred_element_type=jnp.float32)
        centroid_tallies = centroid_tallies + lax.optimization_barrier(jnp.sum(probs.astype(jnp.float32), axis=0))
        return ((centroid_totals, centroid_tallies), restored_vectors)
    init = (jnp.zeros((K, PART_FEATURES), jnp.float32), jnp.zeros((K,), jnp.float32))
    (centroid_totals, centroid_tallies), restored_vectors = lax.scan(step, init, blocks)
    return (restored_vectors.reshape(ROWS, PART_FEATURES), centroid_totals, centroid_tallies)

def reference(vector_window, orthogonal_matrix, centroid_table, sharpness_scale):
    turned_vectors = jnp.dot(vector_window, orthogonal_matrix, preferred_element_type=jnp.float32).astype(jnp.bfloat16)
    pieces = []
    updated = []
    for feature_segment in range(PART_TOTAL):
        restored_vectors, centroid_totals, centroid_tallies = allot_part_vectors(turned_vectors[:, feature_segment * PART_FEATURES:(feature_segment + 1) * PART_FEATURES], centroid_table[feature_segment], sharpness_scale[feature_segment])
        pieces.append(restored_vectors)
        updated.append((centroid_totals + centroid_table[feature_segment].astype(jnp.float32)) / (centroid_tallies[:, None] + 1.0))
    recon = jnp.concatenate(pieces, axis=1)
    new_codebook = jnp.stack(updated, axis=0)
    cross = lax.dot_general(vector_window, recon, (((0,), (0,)), ((), ())), preferred_element_type=jnp.float32)
    cross_cov = cross / math.sqrt(ROWS)
    return (new_codebook, recon, cross_cov)
```

```python
import math

import jax
import jax.numpy as jnp
from jax import lax
from jax.experimental import pallas as pl
from jax.experimental.pallas import tpu as pltpu
from jax.sharding import PartitionSpec as P

LOG2E = math.log2(math.e)
G, F, K, D, R = 4, 256, 2048, 1024, 1024
RB = 256
NB = R // RB
KC = 256
NK = K // KC
f32, bf16 = jnp.float32, jnp.bfloat16
MESH = pl.DeviceIdType.MESH
VM = pl.BlockSpec(memory_space=pltpu.VMEM)


def dot(a, b):
    return jnp.dot(a, b, preferred_element_type=f32)


class Place:
    def __init__(self):
        dp, self.y = lax.axis_index("dp"), lax.axis_index("sub")
        self.x, self.z, self.c = dp // 8, (dp // 2) % 4, dp % 2

    def at(self, axis):
        return {"x": self.x, "y": self.y, "z": self.z}[axis]

    def step(self, axis, d):
        return (self.at(axis) + d) % 4

    def peer(self, axis, d):
        x, y, z = self.x, self.y, self.z
        if axis == "x":
            x = self.step("x", d)
        if axis == "y":
            y = self.step("y", d)
        if axis == "z":
            z = self.step("z", d)
        return ((x * 4 + z) * 2 + self.c, y)

    def sibling(self):
        return ((self.x * 4 + self.z) * 2 + 1 - self.c, self.y)

    def greet(self):
        barrier = pltpu.get_barrier_semaphore()
        for axis in "xyz":
            for d in (1, 2, 3):
                pl.semaphore_signal(barrier, inc=1, device_id=self.peer(axis, d), device_id_type=MESH)
        pl.semaphore_signal(barrier, inc=1, device_id=self.sibling(), device_id_type=MESH)
        pl.semaphore_wait(barrier, 10)


class Sems:
    def __init__(self, send, recv):
        self.send, self.recv, self.n = send, recv, 0

    def copy(self, src, dst, device):
        i = self.n
        self.n += 1
        op = pltpu.make_async_remote_copy(
            src_ref=src, dst_ref=dst, send_sem=self.send.at[i], recv_sem=self.recv.at[i],
            device_id=device, device_id_type=MESH,
        )
        op.start()
        return op


def wait(copies):
    for op in copies:
        op.wait()


GATHER_COPIES = 3 + G * 13


def gather_kernel(own_ref, cb_ref, send, recv, local):
    me = Place()
    sems = Sems(send, recv)
    x, y, z, c = me.x, me.y, me.z, me.c
    mine = pltpu.make_async_copy(own_ref.at[0], cb_ref.at[y, x, z, c], local)
    mine.start()
    me.greet()
    ops = [sems.copy(own_ref.at[0], cb_ref.at[y, x, z, c], me.peer("y", d)) for d in (1, 2, 3)]
    mine.wait()
    wait(ops)
    top, low = pl.ds(0, 32), pl.ds(32, 32)
    first = []
    for g in range(G):
        a, b = cb_ref.at[g, x, z, c, top], cb_ref.at[g, x, z, c, low]
        first.append(
            [sems.copy(a, a, me.peer("x", d)) for d in (1, 2, 3)]
            + [sems.copy(b, b, me.peer("z", d)) for d in (1, 2, 3)]
        )
    second = []
    for g in range(G):
        wait(first[g])
        a, b = cb_ref.at[g, :, z, c, top], cb_ref.at[g, x, :, c, low]
        second.append(
            [sems.copy(a, a, me.peer("z", d)) for d in (1, 2, 3)]
            + [sems.copy(b, b, me.peer("x", d)) for d in (1, 2, 3)]
        )
    last = []
    for g in range(G):
        wait(second[g])
        a = cb_ref.at[g, :, :, c]
        last.append(sems.copy(a, a, me.sibling()))
    wait(last)


def gather(own):
    return pl.pallas_call(
        gather_kernel,
        out_shape=jax.ShapeDtypeStruct((G, 4, 4, 2, 64, F), bf16),
        in_specs=[VM],
        out_specs=VM,
        scratch_shapes=[
            pltpu.SemaphoreType.DMA((GATHER_COPIES,)),
            pltpu.SemaphoreType.DMA((GATHER_COPIES,)),
            pltpu.SemaphoreType.DMA,
        ],
        compiler_params=pltpu.CompilerParams(collective_id=0, has_side_effects=True, vmem_limit_bytes=48 << 20),
        name="gather_codewords",
    )(own)


def compute_kernel(s_ref, x_ref, rot_ref, cb_ref, recon_ref, sums_ref, cnt_ref, cross_ref,
                   y_ref, yt_ref, xt_ref, ct_ref, b_ref, l0, l1, p0, p1):
    for g in range(G):
        cols = pl.ds(g * F, F)

        @pl.loop(0, NB)
        def _(i):
            rows = pl.ds(pl.multiple_of(i * RB, RB), RB)
            y = dot(x_ref[rows, :], rot_ref[:, cols]).astype(bf16)
            y_ref[g, rows, :] = y
            yt_ref[g, :, rows] = y.T

    @pl.loop(0, 4)
    def _(i):
        rows = pl.ds(pl.multiple_of(i * 256, 256), 256)
        xt_ref[:, rows] = x_ref[rows, :].T

    for g in range(G):
        factor = s_ref[g] * LOG2E

        @pl.loop(0, NK)
        def _(j):
            ks = pl.ds(pl.multiple_of(j * KC, KC), KC)
            c = cb_ref[g, ks, :]
            ct_ref[g, :, ks] = c.T
            c32 = c.astype(f32)
            sq = jnp.sum(c32 * c32, axis=1, keepdims=True) * factor
            b_ref[g, ks, :] = jnp.broadcast_to(sq, (KC, 128))

    def logits(g, rb, l):
        yt = yt_ref[g, :, pl.ds(rb * RB, RB)]
        scale = s_ref[g] * (2.0 * LOG2E)
        m = None
        for j in range(NK):
            ks = pl.ds(j * KC, KC)
            v = dot(cb_ref[g, ks, :], yt) * scale - jnp.tile(b_ref[g, ks, :], (1, RB // 128))
            l[ks, :] = v
            w = jnp.max(v.reshape(KC // 8, 8, RB), axis=0)
            m = w if m is None else jnp.maximum(m, w)
        return jnp.max(m, axis=0, keepdims=True)

    def softmax(l, m, p, cols):
        tot = None
        for j in range(NK):
            ks = pl.ds(j * KC, KC)
            e = jnp.exp2(l[ks, :] - m)
            w = jnp.sum(e.reshape(KC // 8, 8, RB), axis=0)
            tot = w if tot is None else tot + w
            p[ks, cols] = e.astype(bf16)
        inv = (1.0 / jnp.sum(tot, axis=0, keepdims=True)).astype(bf16)
        for j in range(NK):
            ks = pl.ds(j * KC, KC)
            p[ks, cols] = p[ks, cols] * inv

    def recon(g, rb, p):
        rows = pl.ds(rb * RB, RB)
        recon_ref[rows, pl.ds(g * F, F)] = dot(ct_ref[g], p[:, rows]).T.astype(bf16)

    def sums(g, q, p):
        n = K // NB
        ks = pl.ds(q * n, n)
        pq = p[ks, :]
        sums_ref[g, ks, :] = dot(pq, y_ref[g]).astype(bf16)
        t = pq[:, :128]
        for i in range(1, R // 128):
            t = t + pq[:, i * 128:(i + 1) * 128]
        ones = jnp.ones((8, 128), bf16)
        row = lax.dot_general(ones, t, (((1,), (1,)), ((), ())), preferred_element_type=f32)
        for i in range(4):
            cnt_ref[q, pl.ds(g * 4 + i, 1), :] = row[:1, i * 128:(i + 1) * 128]

    def cross(g):
        cols = pl.ds(g * F, F)
        cross_ref[:, cols] = dot(xt_ref[...], recon_ref[:, cols]).astype(bf16)

    ls, ps = (l0, l1), (p0, p1)
    steps = [(g, rb) for g in range(G) for rb in range(NB)]
    m = logits(0, 0, l0)
    for t, (g, rb) in enumerate(steps):
        nm = logits(*steps[t + 1], ls[(t + 1) % 2]) if t + 1 < len(steps) else None
        softmax(ls[t % 2], m, ps[g % 2], pl.ds(rb * RB, RB))
        if t:
            pg, pr = steps[t - 1]
            recon(pg, pr, ps[pg % 2])
        if g:
            sums(g - 1, rb, ps[(g - 1) % 2])
            if rb == 1:
                cross(g - 1)
        m = nm
    recon(G - 1, NB - 1, ps[(G - 1) % 2])
    for q in range(NB):
        sums(G - 1, q, ps[(G - 1) % 2])
    cross(G - 1)


def compute(s, x, rot, cb):
    return pl.pallas_call(
        compute_kernel,
        out_shape=[
            jax.ShapeDtypeStruct((R, D), bf16),
            jax.ShapeDtypeStruct((G, K, F), bf16),
            jax.ShapeDtypeStruct((4, 16, 128), f32),
            jax.ShapeDtypeStruct((D, D), bf16),
        ],
        in_specs=[pl.BlockSpec(memory_space=pltpu.SMEM), VM, VM, VM],
        out_specs=[VM, VM, VM, VM],
        scratch_shapes=[
            pltpu.VMEM((G, R, F), bf16), pltpu.VMEM((G, F, R), bf16), pltpu.VMEM((D, R), bf16),
            pltpu.VMEM((G, F, K), bf16), pltpu.VMEM((G, K, 128), f32),
            pltpu.VMEM((K, RB), f32), pltpu.VMEM((K, RB), f32),
            pltpu.VMEM((K, R), bf16), pltpu.VMEM((K, R), bf16),
        ],
        compiler_params=pltpu.CompilerParams(vmem_limit_bytes=62 << 20),
        name="soft_assign",
    )(s, x, rot, cb)


REDUCE_COPIES = G * (1 + 6 + 6) + 3 + (1 + 9) + G * (1 + 6 + 6 + 3 + 6 + 6 + 1)


def add(refs):
    total = refs[0].astype(f32)
    for r in refs[1:]:
        total = total + r.astype(f32)
    return total


def reduce_kernel(own_ref, s_ref, n_ref, u_ref, new_ref, out_ref,
                  s0, r0, r1, t1, r2, t2, r3, n0, n1, m1, n2, m2, n3, m3,
                  u0, v0, v1, w1, v2, w2, v3, send, recv, lsem):
    me = Place()
    sems = Sems(send, recv)
    x, y, z, c = me.x, me.y, me.z, me.c
    top, low = pl.ds(0, 32), pl.ds(32, 32)
    left, right = pl.ds(0, 128), pl.ds(128, 128)
    ring = (1, 2, 3)
    me.greet()

    a0 = [sems.copy(s_ref.at[g, :, :, 1 - c], r0.at[g], me.sibling()) for g in range(G)]
    b0 = [sems.copy(u_ref.at[1 - c, :, :, :, pl.ds(g * F, F)], v0.at[g], me.sibling()) for g in range(G)]
    k0 = [sems.copy(n_ref, n0, me.sibling())]

    a1, b1 = [], []
    for g in range(G):
        wait([a0[g]])

        @pl.loop(0, 4)
        def _(i):
            s0[g, i] = add([s_ref[g, i, :, c], r0[g, i]]).astype(bf16)

        a1.append(
            [sems.copy(s0.at[g, me.step("x", d), :, top], r1.at[g, 0, d - 1], me.peer("x", d)) for d in ring]
            + [sems.copy(s0.at[g, :, me.step("z", d), low], r1.at[g, 1, d - 1], me.peer("z", d)) for d in ring]
        )
        wait([b0[g]])

        @pl.loop(0, 4)
        def _(i):
            u0[g, i] = add([u_ref[c, i, :, :, pl.ds(g * F, F)], v0[g, i]]).astype(bf16)

        b1.append(
            [sems.copy(u0.at[g, me.step("x", d), :, :, left], v1.at[g, 0, d - 1], me.peer("x", d)) for d in ring]
            + [sems.copy(u0.at[g, me.step("z", d), :, :, right], v1.at[g, 1, d - 1], me.peer("z", d)) for d in ring]
        )
    wait(k0)
    m1[...] = n_ref[...] + n0[...]
    k1 = [sems.copy(m1.at[me.step("x", d)], n1.at[d - 1], me.peer("x", d)) for d in ring]

    a2, b2 = [], []
    for g in range(G):
        wait(a1[g])
        t1[g, 0] = add([s0[g, x, :, top]] + [r1[g, 0, i] for i in range(3)]).astype(bf16)
        t1[g, 1] = add([s0[g, :, z, low]] + [r1[g, 1, i] for i in range(3)]).astype(bf16)
        a2.append(
            [sems.copy(t1.at[g, 0, me.step("z", d)], r2.at[g, 0, d - 1], me.peer("z", d)) for d in ring]
            + [sems.copy(t1.at[g, 1, me.step("x", d)], r2.at[g, 1, d - 1], me.peer("x", d)) for d in ring]
        )
        wait(b1[g])
        w1[g, 0] = add([u0[g, x, :, :, left]] + [v1[g, 0, i] for i in range(3)]).astype(bf16)
        w1[g, 1] = add([u0[g, z, :, :, right]] + [v1[g, 1, i] for i in range(3)]).astype(bf16)
        b2.append(
            [sems.copy(w1.at[g, 0, me.step("z", d)], v2.at[g, 0, d - 1], me.peer("z", d)) for d in ring]
            + [sems.copy(w1.at[g, 1, me.step("x", d)], v2.at[g, 1, d - 1], me.peer("x", d)) for d in ring]
        )
    wait(k1)
    m2[...] = m1[x] + n1[0] + n1[1] + n1[2]
    k2 = [sems.copy(m2, n2.at[d - 1], me.peer("z", d)) for d in ring]

    b3 = []
    for g in range(G):
        wait(a2[g])
        t2[g, top] = add([t1[g, 0, z]] + [r2[g, 0, i] for i in range(3)]).astype(bf16)
        t2[g, low] = add([t1[g, 1, x]] + [r2[g, 1, i] for i in range(3)]).astype(bf16)
        wait(b2[g])
        v3[g, y, 0] = add([w1[g, 0, z]] + [v2[g, 0, i] for i in range(3)]).astype(bf16)
        v3[g, y, 1] = add([w1[g, 1, x]] + [v2[g, 1, i] for i in range(3)]).astype(bf16)
        b3.append([sems.copy(v3.at[g, y], v3.at[g, y], me.peer("y", d)) for d in ring])
    a3 = [sems.copy(t2.at[me.step("y", d)], r3.at[d - 1], me.peer("y", d)) for d in ring]
    wait(k2)
    m3[...] = m2[...] + n2[0] + n2[1] + n2[2]
    k3 = [sems.copy(m3, n3.at[d - 1], me.peer("y", d)) for d in ring]

    b4 = []
    for g in range(G):
        wait(b3[g])
        one, two = pl.ds(g * F, 128), pl.ds(g * F + 128, 128)
        out_ref[c, x, z, :, one] = add([v3[g, i, 0] for i in range(4)]).astype(bf16)
        out_ref[c, z, x, :, two] = add([v3[g, i, 1] for i in range(4)]).astype(bf16)
        e, f = out_ref.at[c, x, z, :, one], out_ref.at[c, z, x, :, two]
        b4.append(
            [sems.copy(e, e, me.peer("z", d)) for d in ring] + [sems.copy(f, f, me.peer("x", d)) for d in ring]
        )

    wait(a3)
    wait(k3)
    sums = add([t2[y]] + [r3[i] for i in range(3)])
    rows = m3[...] + n3[0] + n3[1] + n3[2]
    at_row = lax.broadcasted_iota(jnp.int32, (16, 128), 0) == y * 4 + z
    row = jnp.sum(jnp.where(at_row, rows, 0.0), axis=0, keepdims=True)
    spread = jnp.broadcast_to(row, (64, 128))
    lane, sub = lax.broadcasted_iota(jnp.int32, (64, 128), 1), lax.broadcasted_iota(jnp.int32, (64, 128), 0)
    count = jnp.sum(jnp.where(lane == sub + c * 64, spread, 0.0), axis=1, keepdims=True)
    new_ref[0] = (sums + own_ref[0].astype(f32)) / (count + 1.0)

    b5 = []
    for g in range(G):
        wait(b4[g])
        one, two = pl.ds(g * F, 128), pl.ds(g * F + 128, 128)
        e, f = out_ref.at[c, x, :, :, one], out_ref.at[c, z, :, :, two]
        b5.append(
            [sems.copy(e, e, me.peer("x", d)) for d in ring] + [sems.copy(f, f, me.peer("z", d)) for d in ring]
        )
    b6 = []
    for g in range(G):
        wait(b5[g])
        e = out_ref.at[c, :, :, :, pl.ds(g * F, F)]
        b6.append(sems.copy(e, e, me.sibling()))
    wait(b6)


def reduce(own, sums, counts, cross):
    return pl.pallas_call(
        reduce_kernel,
        out_shape=[
            jax.ShapeDtypeStruct((1, 64, F), f32),
            jax.ShapeDtypeStruct((2, 4, 4, 32, D), bf16),
        ],
        in_specs=[VM] * 4,
        out_specs=[VM] * 2,
        scratch_shapes=[
            pltpu.VMEM((G, 4, 4, 64, F), bf16), pltpu.VMEM((G, 4, 4, 64, F), bf16),
            pltpu.VMEM((G, 2, 3, 4, 32, F), bf16), pltpu.VMEM((G, 2, 4, 32, F), bf16),
            pltpu.VMEM((G, 2, 3, 32, F), bf16), pltpu.VMEM((G, 64, F), bf16), pltpu.VMEM((3, 64, F), bf16),
            pltpu.VMEM((4, 16, 128), f32), pltpu.VMEM((3, 16, 128), f32), pltpu.VMEM((4, 16, 128), f32),
            pltpu.VMEM((3, 16, 128), f32), pltpu.VMEM((16, 128), f32), pltpu.VMEM((3, 16, 128), f32),
            pltpu.VMEM((16, 128), f32),
            pltpu.VMEM((G, 4, 4, 32, F), bf16), pltpu.VMEM((G, 4, 4, 32, F), bf16),
            pltpu.VMEM((G, 2, 3, 4, 32, 128), bf16), pltpu.VMEM((G, 2, 4, 32, 128), bf16),
            pltpu.VMEM((G, 2, 3, 32, 128), bf16), pltpu.VMEM((16, 128), bf16),
            pltpu.VMEM((G, 4, 2, 32, 128), bf16),
            pltpu.SemaphoreType.DMA((REDUCE_COPIES,)),
            pltpu.SemaphoreType.DMA((REDUCE_COPIES,)),
            pltpu.SemaphoreType.DMA,
        ],
        compiler_params=pltpu.CompilerParams(collective_id=1, has_side_effects=True, vmem_limit_bytes=48 << 20),
        name="reduce_all",
    )(own, sums, counts, cross)


def body(vector_window, orthogonal_matrix, centroid_table, sharpness_scale):
    codewords = gather(centroid_table)
    recon, sums, counts, cross = compute(
        sharpness_scale, vector_window, orthogonal_matrix, codewords.reshape(G, K, F)
    )
    new_codebook, total = reduce(
        centroid_table, sums.reshape(G, 4, 4, 2, 64, F), counts, cross.reshape(2, 4, 4, 32, D)
    )
    total_rows = R * lax.axis_size("dp") * lax.axis_size("sub")
    cross_cov = total.reshape(D, D).astype(f32) * (1.0 / math.sqrt(total_rows))
    return (new_codebook, recon, cross_cov)


def solution(mesh):
    placed = (P(("dp", "sub"), None), P(), P("sub", "dp", None), P())
    return jax.shard_map(
        body,
        mesh=mesh,
        in_specs=placed,
        out_specs=(P("sub", "dp", None), P(("dp", "sub"), None), P()),
        check_vma=False,
    )
```

```python
import math

import jax
import jax.numpy as jnp
from jax import lax
from jax.experimental import pallas as pl
from jax.experimental.pallas import tpu as pltpu
from jax.sharding import PartitionSpec as P

LOG2E = math.log2(math.e)
G, F, K, D, R = 4, 256, 2048, 1024, 1024
RB = 256
NB = R // RB
KC = 256
NK = K // KC
f32, bf16 = jnp.float32, jnp.bfloat16
MESH = pl.DeviceIdType.MESH
VM = pl.BlockSpec(memory_space=pltpu.VMEM)


def dot(a, b):
    return jnp.dot(a, b, preferred_element_type=f32)


class Place:
    def __init__(self):
        dp, self.y = lax.axis_index("dp"), lax.axis_index("sub")
        self.x, self.z, self.c = dp // 8, (dp // 2) % 4, dp % 2

    def at(self, axis):
        return {"x": self.x, "y": self.y, "z": self.z}[axis]

    def step(self, axis, d):
        return (self.at(axis) + d) % 4

    def peer(self, axis, d):
        x, y, z = self.x, self.y, self.z
        if axis == "x":
            x = self.step("x", d)
        if axis == "y":
            y = self.step("y", d)
        if axis == "z":
            z = self.step("z", d)
        return ((x * 4 + z) * 2 + self.c, y)

    def sibling(self):
        return ((self.x * 4 + self.z) * 2 + 1 - self.c, self.y)

    def greet(self):
        barrier = pltpu.get_barrier_semaphore()
        for axis in "xyz":
            for d in (1, 2, 3):
                pl.semaphore_signal(barrier, inc=1, device_id=self.peer(axis, d), device_id_type=MESH)
        pl.semaphore_signal(barrier, inc=1, device_id=self.sibling(), device_id_type=MESH)
        pl.semaphore_wait(barrier, 10)


class Sems:
    def __init__(self, send, recv):
        self.send, self.recv, self.n = send, recv, 0

    def copy(self, src, dst, device):
        i = self.n
        self.n += 1
        op = pltpu.make_async_remote_copy(
            src_ref=src, dst_ref=dst, send_sem=self.send.at[i], recv_sem=self.recv.at[i],
            device_id=device, device_id_type=MESH,
        )
        op.start()
        return op


def wait(copies):
    for op in copies:
        op.wait()


RING = (1, 2, 3)
TOP, LOW = pl.ds(0, 32), pl.ds(32, 32)


def add(refs):
    total = refs[0].astype(f32)
    for r in refs[1:]:
        total = total + r.astype(f32)
    return total


def kernel(s_ref, x_hbm, rot_hbm, own_ref, new_ref, recon_hbm, out_ref,
           x_ref, rot_ref, cb_ref, recon_ref, s_sum, u_ref, n_ref,
           y_ref, yt_ref, xt_ref, ct0, ct1, b0, b1, l0, l1, p0, p1,
           s0, r0, r1, t1, r2, t2, r3, n0, n1, m1, n2, m2, n3, m3,
           u0, v0, v1, w1, v2, w2, v3, send, recv, lsem):
    me = Place()
    sems = Sems(send, recv)
    x, y, z, c = me.x, me.y, me.z, me.c

    def to(axis, pairs):
        return [sems.copy(*pairs(d), me.peer(axis, d)) for d in RING]

    load_x = pltpu.make_async_copy(x_hbm, x_ref, lsem.at[0])
    load_rot = pltpu.make_async_copy(rot_hbm, rot_ref, lsem.at[1])
    mine = pltpu.make_async_copy(own_ref.at[0], cb_ref.at[y, x, z, c], lsem.at[2])
    load_x.start()
    load_rot.start()
    mine.start()
    me.greet()


    def gather_own():
        return to("y", lambda d: (own_ref.at[0], cb_ref.at[y, x, z, c]))

    def gather_first(g):
        a, b = cb_ref.at[g, x, z, c, TOP], cb_ref.at[g, x, z, c, LOW]
        return to("x", lambda d: (a, a)) + to("z", lambda d: (b, b))

    def gather_second(g):
        a, b = cb_ref.at[g, :, z, c, TOP], cb_ref.at[g, x, :, c, LOW]
        return to("z", lambda d: (a, a)) + to("x", lambda d: (b, b))

    def gather_core(g):
        a = cb_ref.at[g, :, :, c]
        return [sems.copy(a, a, me.sibling())]

    def sums_task(g):
        ops = [sems.copy(s_sum.at[g, :, :, 1 - c], r0.at[g], me.sibling())]
        yield
        wait(ops)

        @pl.loop(0, 4)
        def _(i):
            s0[g, i] = add([s_sum[g, i, :, c], r0[g, i]]).astype(bf16)

        ops = to("x", lambda d: (s0.at[g, me.step("x", d), :, TOP], r1.at[g, 0, d - 1]))
        ops += to("z", lambda d: (s0.at[g, :, me.step("z", d), LOW], r1.at[g, 1, d - 1]))
        yield
        wait(ops)
        t1[g, 0] = add([s0[g, x, :, TOP]] + [r1[g, 0, i] for i in range(3)]).astype(bf16)
        t1[g, 1] = add([s0[g, :, z, LOW]] + [r1[g, 1, i] for i in range(3)]).astype(bf16)
        ops = to("z", lambda d: (t1.at[g, 0, me.step("z", d)], r2.at[g, 0, d - 1]))
        ops += to("x", lambda d: (t1.at[g, 1, me.step("x", d)], r2.at[g, 1, d - 1]))
        yield
        wait(ops)
        t2[g, TOP] = add([t1[g, 0, z]] + [r2[g, 0, i] for i in range(3)]).astype(bf16)
        t2[g, LOW] = add([t1[g, 1, x]] + [r2[g, 1, i] for i in range(3)]).astype(bf16)

    def counts_task():
        ops = [sems.copy(n_ref, n0, me.sibling())]
        yield
        wait(ops)
        m1[...] = n_ref[...] + n0[...]
        ops = to("x", lambda d: (m1.at[me.step("x", d)], n1.at[d - 1]))
        yield
        wait(ops)
        m2[...] = m1[x] + n1[0] + n1[1] + n1[2]
        ops = to("z", lambda d: (m2, n2.at[d - 1]))
        yield
        wait(ops)
        m3[...] = m2[...] + n2[0] + n2[1] + n2[2]

    def owner_task():
        ops = to("y", lambda d: (t2.at[me.step("y", d)], r3.at[d - 1]))
        ops += to("y", lambda d: (m3, n3.at[d - 1]))
        yield
        wait(ops)
        sums = add([t2[y]] + [r3[i] for i in range(3)])
        rows = m3[...] + n3[0] + n3[1] + n3[2]
        at_row = lax.broadcasted_iota(jnp.int32, (16, 128), 0) == y * 4 + z
        row = jnp.sum(jnp.where(at_row, rows, 0.0), axis=0, keepdims=True)
        spread = jnp.broadcast_to(row, (64, 128))
        lane, sub = lax.broadcasted_iota(jnp.int32, (64, 128), 1), lax.broadcasted_iota(jnp.int32, (64, 128), 0)
        count = jnp.sum(jnp.where(lane == sub + c * 64, spread, 0.0), axis=1, keepdims=True)
        new_ref[0] = (sums + own_ref[0].astype(f32)) / (count + 1.0)

    def cross_task(g):
        one, two = pl.ds(g * F, 128), pl.ds(g * F + 128, 128)
        left, right = pl.ds(0, 128), pl.ds(128, 128)
        ops = [sems.copy(u_ref.at[1 - c, :, :, :, pl.ds(g * F, F)], v0.at[g], me.sibling())]
        yield
        wait(ops)

        @pl.loop(0, 4)
        def _(i):
            u0[g, i] = add([u_ref[c, i, :, :, pl.ds(g * F, F)], v0[g, i]]).astype(bf16)

        ops = to("x", lambda d: (u0.at[g, me.step("x", d), :, :, left], v1.at[g, 0, d - 1]))
        ops += to("z", lambda d: (u0.at[g, me.step("z", d), :, :, right], v1.at[g, 1, d - 1]))
        yield
        wait(ops)
        w1[g, 0] = add([u0[g, x, :, :, left]] + [v1[g, 0, i] for i in range(3)]).astype(bf16)
        w1[g, 1] = add([u0[g, z, :, :, right]] + [v1[g, 1, i] for i in range(3)]).astype(bf16)
        ops = to("z", lambda d: (w1.at[g, 0, me.step("z", d)], v2.at[g, 0, d - 1]))
        ops += to("x", lambda d: (w1.at[g, 1, me.step("x", d)], v2.at[g, 1, d - 1]))
        yield
        wait(ops)
        v3[g, y, 0] = add([w1[g, 0, z]] + [v2[g, 0, i] for i in range(3)]).astype(bf16)
        v3[g, y, 1] = add([w1[g, 1, x]] + [v2[g, 1, i] for i in range(3)]).astype(bf16)
        ops = to("y", lambda d: (v3.at[g, y], v3.at[g, y]))
        yield
        wait(ops)
        out_ref[c, x, z, :, one] = add([v3[g, i, 0] for i in range(4)]).astype(bf16)
        out_ref[c, z, x, :, two] = add([v3[g, i, 1] for i in range(4)]).astype(bf16)
        e, f = out_ref.at[c, x, z, :, one], out_ref.at[c, z, x, :, two]
        ops = to("z", lambda d: (e, e)) + to("x", lambda d: (f, f))
        yield
        wait(ops)
        h, i = out_ref.at[c, x, :, :, one], out_ref.at[c, z, :, :, two]
        ops = to("x", lambda d: (h, h)) + to("z", lambda d: (i, i))
        yield
        wait(ops)
        k = out_ref.at[c, :, :, :, pl.ds(g * F, F)]
        ops = [sems.copy(k, k, me.sibling())]
        yield
        wait(ops)


    cts, bs, ls, ps = (ct0, ct1), (b0, b1), (l0, l1), (p0, p1)

    def rotate():
        @pl.loop(0, NB)
        def _(i):
            rows = pl.ds(pl.multiple_of(i * RB, RB), RB)
            for g in range(G):
                v = dot(x_ref[rows, :], rot_ref[:, pl.ds(g * F, F)]).astype(bf16)
                y_ref[g, rows, :] = v
                yt_ref[g, :, rows] = v.T

    def turn_x():
        @pl.loop(0, 4)
        def _(i):
            rows = pl.ds(pl.multiple_of(i * 256, 256), 256)
            xt_ref[:, rows] = x_ref[rows, :].T

    def words(g, j):
        return cb_ref[g, j // 2, pl.ds((j % 2) * 2, 2)].reshape(KC, F)

    def prepare(g):
        factor = s_ref[g] * LOG2E
        for j in range(NK):
            ks = pl.ds(j * KC, KC)
            v = words(g, j)
            cts[g % 2][:, ks] = v.T
            v32 = v.astype(f32)
            sq = jnp.sum(v32 * v32, axis=1, keepdims=True) * factor
            bs[g % 2][ks, :] = jnp.broadcast_to(sq, (KC, 128))

    def logits(g, rb, l):
        yt = yt_ref[g, :, pl.ds(rb * RB, RB)]
        scale = s_ref[g] * (2.0 * LOG2E)
        m = None
        for j in range(NK):
            ks = pl.ds(j * KC, KC)
            v = dot(words(g, j), yt) * scale - jnp.tile(bs[g % 2][ks, :], (1, RB // 128))
            l[ks, :] = v
            w = jnp.max(v.reshape(KC // 8, 8, RB), axis=0)
            m = w if m is None else jnp.maximum(m, w)
        return jnp.max(m, axis=0, keepdims=True)

    def softmax(l, m, p, cols):
        tot = None
        for j in range(NK):
            ks = pl.ds(j * KC, KC)
            e = jnp.exp2(l[ks, :] - m)
            w = jnp.sum(e.reshape(KC // 8, 8, RB), axis=0)
            tot = w if tot is None else tot + w
            p[ks, cols] = e.astype(bf16)
        inv = (1.0 / jnp.sum(tot, axis=0, keepdims=True)).astype(bf16)
        for j in range(NK):
            ks = pl.ds(j * KC, KC)
            p[ks, cols] = p[ks, cols] * inv

    def recon(g, rb, p):
        rows = pl.ds(rb * RB, RB)
        recon_ref[rows, pl.ds(g * F, F)] = dot(cts[g % 2][...], p[:, rows]).T.astype(bf16)

    def sums(g, q, p):
        n = K // NB
        pq = p[pl.ds(q * n, n), :]
        s_sum[g, q] = dot(pq, y_ref[g]).astype(bf16).reshape(4, 2, 64, F)
        t = pq[:, :128]
        for i in range(1, R // 128):
            t = t + pq[:, i * 128:(i + 1) * 128]
        ones = jnp.ones((8, 128), bf16)
        row = lax.dot_general(ones, t, (((1,), (1,)), ((), ())), preferred_element_type=f32)
        for i in range(4):
            n_ref[q, pl.ds(g * 4 + i, 1), :] = row[:1, i * 128:(i + 1) * 128]

    def cross(g):
        cols = pl.ds(g * F, F)
        u_ref[:, :, :, :, cols] = dot(xt_ref[...], recon_ref[:, cols]).astype(bf16).reshape(2, 4, 4, 32, F)

    def store(g):
        cols = pl.ds(g * F, F)
        op = pltpu.make_async_copy(recon_ref.at[:, cols], recon_hbm.at[:, cols], lsem.at[3 + g])
        op.start()
        return op


    stage_y = gather_own()
    load_x.wait()
    load_rot.wait()
    mine.wait()
    wait(stage_y)
    first = [gather_first(0)]
    rotate()
    wait(first[0])
    second = [gather_second(0)]
    first.append(gather_first(1))
    turn_x()
    wait(first[1])
    wait(second[0])
    last = [gather_core(0)]
    second.append(gather_second(1))
    first.append(gather_first(2))
    wait(last[0])
    prepare(0)

    stores, tasks = [], []

    def tick(now):
        for task in list(tasks):
            if now >= task[1]:
                task[1] = now + 2
                if next(task[0], task) is task:
                    tasks.remove(task)

    def begin(now, task):
        tasks.append([task, now + 2])
        next(task)

    steps = [(g, rb) for g in range(G) for rb in range(NB)]
    m = logits(0, 0, l0)
    for t, (g, rb) in enumerate(steps):
        if g + 1 < G:
            if rb == 1:
                wait(second[g + 1])
                last.append(gather_core(g + 1))
                if g + 2 < G:
                    wait(first[g + 2])
                    second.append(gather_second(g + 2))
                if g + 3 < G:
                    first.append(gather_first(g + 3))
            if rb == 2:
                wait(last[g + 1])
                prepare(g + 1)
        nm = logits(*steps[t + 1], ls[(t + 1) % 2]) if t + 1 < len(steps) else None
        softmax(ls[t % 2], m, ps[g % 2], pl.ds(rb * RB, RB))
        if t:
            pg, pr = steps[t - 1]
            recon(pg, pr, ps[pg % 2])
        if g:
            sums(g - 1, rb, ps[(g - 1) % 2])
            if rb == 0:
                stores.append(store(g - 1))
                cross(g - 1)
        tick(t)
        if g and rb == 0:
            begin(t, cross_task(g - 1))
        if g and rb == 3:
            begin(t, sums_task(g - 1))
        m = nm
    recon(G - 1, NB - 1, ps[(G - 1) % 2])
    stores.append(store(G - 1))
    cross(G - 1)
    begin(0, cross_task(G - 1))
    for q in range(NB):
        sums(G - 1, q, ps[(G - 1) % 2])
    begin(0, sums_task(G - 1))
    begin(0, counts_task())
    reduced = [task for task in tasks]
    owner = None
    while tasks:
        tick(1 << 20)
        for task in tasks:
            task[1] = 0
        if owner is None and not any(t in tasks for t in reduced[-2:]):
            owner = owner_task()
            begin(0, owner)
    for op in stores:
        op.wait()


COPIES = 3 + G * 13 + G * 13 + 10 + 6 + G * 29


def call(s, x, rot, own):
    any_place = pl.BlockSpec(memory_space=pl.ANY)
    return pl.pallas_call(
        kernel,
        out_shape=[
            jax.ShapeDtypeStruct((1, 64, F), f32),
            jax.ShapeDtypeStruct((R, D), bf16),
            jax.ShapeDtypeStruct((2, 4, 4, 32, D), bf16),
        ],
        in_specs=[pl.BlockSpec(memory_space=pltpu.SMEM), any_place, any_place, VM],
        out_specs=[VM, any_place, VM],
        scratch_shapes=[
            pltpu.VMEM((R, D), bf16), pltpu.VMEM((D, D), bf16), pltpu.VMEM((G, 4, 4, 2, 64, F), bf16),
            pltpu.VMEM((R, D), bf16), pltpu.VMEM((G, 4, 4, 2, 64, F), bf16), pltpu.VMEM((2, 4, 4, 32, D), bf16),
            pltpu.VMEM((4, 16, 128), f32),
            pltpu.VMEM((G, R, F), bf16), pltpu.VMEM((G, F, R), bf16), pltpu.VMEM((D, R), bf16),
            pltpu.VMEM((F, K), bf16), pltpu.VMEM((F, K), bf16),
            pltpu.VMEM((K, 128), f32), pltpu.VMEM((K, 128), f32),
            pltpu.VMEM((K, RB), f32), pltpu.VMEM((K, RB), f32),
            pltpu.VMEM((K, R), bf16), pltpu.VMEM((K, R), bf16),
            pltpu.VMEM((G, 4, 4, 64, F), bf16), pltpu.VMEM((G, 4, 4, 64, F), bf16),
            pltpu.VMEM((G, 2, 3, 4, 32, F), bf16), pltpu.VMEM((G, 2, 4, 32, F), bf16),
            pltpu.VMEM((G, 2, 3, 32, F), bf16), pltpu.VMEM((G, 64, F), bf16), pltpu.VMEM((3, 64, F), bf16),
            pltpu.VMEM((4, 16, 128), f32), pltpu.VMEM((3, 16, 128), f32), pltpu.VMEM((4, 16, 128), f32),
            pltpu.VMEM((3, 16, 128), f32), pltpu.VMEM((16, 128), f32), pltpu.VMEM((3, 16, 128), f32),
            pltpu.VMEM((16, 128), f32),
            pltpu.VMEM((G, 4, 4, 32, F), bf16), pltpu.VMEM((G, 4, 4, 32, F), bf16),
            pltpu.VMEM((G, 2, 3, 4, 32, 128), bf16), pltpu.VMEM((G, 2, 4, 32, 128), bf16),
            pltpu.VMEM((G, 2, 3, 32, 128), bf16), pltpu.VMEM((16, 128), bf16),
            pltpu.VMEM((G, 4, 2, 32, 128), bf16),
            pltpu.SemaphoreType.DMA((COPIES,)),
            pltpu.SemaphoreType.DMA((COPIES,)),
            pltpu.SemaphoreType.DMA((3 + G,)),
        ],
        compiler_params=pltpu.CompilerParams(collective_id=0, has_side_effects=True, vmem_limit_bytes=63 << 20),
        name="quantizer_step",
    )(s, x, rot, own)


def body(vector_window, orthogonal_matrix, centroid_table, sharpness_scale):
    new_codebook, recon, total = call(sharpness_scale, vector_window, orthogonal_matrix, centroid_table)
    total_rows = R * lax.axis_size("dp") * lax.axis_size("sub")
    cross_cov = total.reshape(D, D).astype(f32) * (1.0 / math.sqrt(total_rows))
    return (new_codebook, recon, cross_cov)


def solution(mesh):
    placed = (P(("dp", "sub"), None), P(), P("sub", "dp", None), P())
    return jax.shard_map(
        body,
        mesh=mesh,
        in_specs=placed,
        out_specs=(P("sub", "dp", None), P(("dp", "sub"), None), P()),
        check_vma=False,
    )
```

```python
import functools
import math

import jax
import jax.numpy as jnp
from jax import lax
from jax.experimental import pallas as pl
from jax.experimental.pallas import tpu as pltpu
from jax.sharding import PartitionSpec as P

LOG2E = math.log2(math.e)
G, F, K, D, R = 4, 256, 2048, 1024, 1024
RB = 256
NB = R // RB
KC = 256
NK = K // KC
f32, bf16 = jnp.float32, jnp.bfloat16
MESH = pl.DeviceIdType.MESH
VM = pl.BlockSpec(memory_space=pltpu.VMEM)


def dot(a, b):
    return jnp.dot(a, b, preferred_element_type=f32)


class Place:
    def __init__(self):
        dp, self.y = lax.axis_index("dp"), lax.axis_index("sub")
        self.x, self.z, self.c = dp // 8, (dp // 2) % 4, dp % 2

    def at(self, axis):
        return {"x": self.x, "y": self.y, "z": self.z}[axis]

    def step(self, axis, d):
        return (self.at(axis) + d) % 4

    def peer(self, axis, d):
        x, y, z = self.x, self.y, self.z
        if axis == "x":
            x = self.step("x", d)
        if axis == "y":
            y = self.step("y", d)
        if axis == "z":
            z = self.step("z", d)
        return ((x * 4 + z) * 2 + self.c, y)

    def sibling(self):
        return ((self.x * 4 + self.z) * 2 + 1 - self.c, self.y)

    def greet(self):
        barrier = pltpu.get_barrier_semaphore()
        for axis in "xyz":
            for d in (1, 2, 3):
                pl.semaphore_signal(barrier, inc=1, device_id=self.peer(axis, d), device_id_type=MESH)
        pl.semaphore_signal(barrier, inc=1, device_id=self.sibling(), device_id_type=MESH)
        pl.semaphore_wait(barrier, 10)


class Sems:
    def __init__(self, send, recv):
        self.send, self.recv, self.n = send, recv, 0

    def copy(self, src, dst, device):
        i = self.n
        self.n += 1
        op = pltpu.make_async_remote_copy(
            src_ref=src, dst_ref=dst, send_sem=self.send.at[i], recv_sem=self.recv.at[i],
            device_id=device, device_id_type=MESH,
        )
        op.start()
        return op


def wait(copies):
    for op in copies:
        op.wait()


RING = (1, 2, 3)
TOP, LOW = pl.ds(0, 32), pl.ds(32, 32)


def add(refs):
    total = refs[0].astype(f32)
    for r in refs[1:]:
        total = total + r.astype(f32)
    return total


def kernel(s_ref, x_hbm, rot_hbm, own_ref, new_ref, recon_ref, out_ref,
           rot_ref, cb_ref, s_sum, u_ref, n_ref,
           y_ref, yt_ref, xt_ref, ct0, ct1, b0, b1, l0, l1, p0, p1,
           s0, r0, r1, t1, r2, t2, r3, n0, n1, m1, n2, m2, n3, m3,
           u0, v0, v1, w1, v2, w2, v3, send, recv, lsem):
    me = Place()
    sems = Sems(send, recv)
    x, y, z, c = me.x, me.y, me.z, me.c

    def to(axis, pairs):
        return [sems.copy(*pairs(d), me.peer(axis, d)) for d in RING]

    x_ref = recon_ref
    load_x = pltpu.make_async_copy(x_hbm, x_ref, lsem.at[0])
    load_rot = pltpu.make_async_copy(rot_hbm, rot_ref, lsem.at[1])
    mine = pltpu.make_async_copy(own_ref.at[0], cb_ref.at[y, x, z, c], lsem.at[2])
    load_x.start()
    load_rot.start()
    mine.start()
    me.greet()


    def gather_own():
        return to("y", lambda d: (own_ref.at[0], cb_ref.at[y, x, z, c]))

    def gather_first(g):
        a, b = cb_ref.at[g, x, z, c, TOP], cb_ref.at[g, x, z, c, LOW]
        return to("x", lambda d: (a, a)) + to("z", lambda d: (b, b))

    def gather_second(g):
        a, b = cb_ref.at[g, :, z, c, TOP], cb_ref.at[g, x, :, c, LOW]
        return to("z", lambda d: (a, a)) + to("x", lambda d: (b, b))

    def gather_core(g):
        a = cb_ref.at[g, :, :, c]
        return [sems.copy(a, a, me.sibling())]

    def sums_task(g):
        ops = [sems.copy(s_sum.at[g, :, :, 1 - c], r0.at[g], me.sibling())]
        yield
        wait(ops)

        @pl.loop(0, 4)
        def _(i):
            s0[g, i] = add([s_sum[g, i, :, c], r0[g, i]]).astype(bf16)

        ops = to("x", lambda d: (s0.at[g, me.step("x", d), :, TOP], r1.at[g, 0, d - 1]))
        ops += to("z", lambda d: (s0.at[g, :, me.step("z", d), LOW], r1.at[g, 1, d - 1]))
        yield
        wait(ops)
        t1[g, 0] = add([s0[g, x, :, TOP]] + [r1[g, 0, i] for i in range(3)]).astype(bf16)
        t1[g, 1] = add([s0[g, :, z, LOW]] + [r1[g, 1, i] for i in range(3)]).astype(bf16)
        ops = to("z", lambda d: (t1.at[g, 0, me.step("z", d)], r2.at[g, 0, d - 1]))
        ops += to("x", lambda d: (t1.at[g, 1, me.step("x", d)], r2.at[g, 1, d - 1]))
        yield
        wait(ops)
        t2[g, TOP] = add([t1[g, 0, z]] + [r2[g, 0, i] for i in range(3)]).astype(bf16)
        t2[g, LOW] = add([t1[g, 1, x]] + [r2[g, 1, i] for i in range(3)]).astype(bf16)

    def counts_task():
        ops = [sems.copy(n_ref, n0, me.sibling())]
        yield
        wait(ops)
        m1[...] = n_ref[...] + n0[...]
        ops = to("x", lambda d: (m1.at[me.step("x", d)], n1.at[d - 1]))
        yield
        wait(ops)
        m2[...] = m1[x] + n1[0] + n1[1] + n1[2]
        ops = to("z", lambda d: (m2, n2.at[d - 1]))
        yield
        wait(ops)
        m3[...] = m2[...] + n2[0] + n2[1] + n2[2]

    def owner_task():
        ops = to("y", lambda d: (t2.at[me.step("y", d)], r3.at[d - 1]))
        ops += to("y", lambda d: (m3, n3.at[d - 1]))
        yield
        wait(ops)
        sums = add([t2[y]] + [r3[i] for i in range(3)])
        rows = m3[...] + n3[0] + n3[1] + n3[2]
        at_row = lax.broadcasted_iota(jnp.int32, (16, 128), 0) == y * 4 + z
        row = jnp.sum(jnp.where(at_row, rows, 0.0), axis=0, keepdims=True)
        spread = jnp.broadcast_to(row, (64, 128))
        lane, sub = lax.broadcasted_iota(jnp.int32, (64, 128), 1), lax.broadcasted_iota(jnp.int32, (64, 128), 0)
        count = jnp.sum(jnp.where(lane == sub + c * 64, spread, 0.0), axis=1, keepdims=True)
        new_ref[0] = (sums + own_ref[0].astype(f32)) / (count + 1.0)

    def cross_task(g):
        one, two = pl.ds(g * F, 128), pl.ds(g * F + 128, 128)
        left, right = pl.ds(0, 128), pl.ds(128, 128)
        ops = [sems.copy(u_ref.at[1 - c, :, :, :, pl.ds(g * F, F)], v0.at[g], me.sibling())]
        yield
        wait(ops)

        @pl.loop(0, 4)
        def _(i):
            u0[g, i] = add([u_ref[c, i, :, :, pl.ds(g * F, F)], v0[g, i]]).astype(bf16)

        ops = to("x", lambda d: (u0.at[g, me.step("x", d), :, :, left], v1.at[g, 0, d - 1]))
        ops += to("z", lambda d: (u0.at[g, me.step("z", d), :, :, right], v1.at[g, 1, d - 1]))
        yield
        wait(ops)
        w1[g, 0] = add([u0[g, x, :, :, left]] + [v1[g, 0, i] for i in range(3)]).astype(bf16)
        w1[g, 1] = add([u0[g, z, :, :, right]] + [v1[g, 1, i] for i in range(3)]).astype(bf16)
        ops = to("z", lambda d: (w1.at[g, 0, me.step("z", d)], v2.at[g, 0, d - 1]))
        ops += to("x", lambda d: (w1.at[g, 1, me.step("x", d)], v2.at[g, 1, d - 1]))
        yield
        wait(ops)
        v3[g, y, 0] = add([w1[g, 0, z]] + [v2[g, 0, i] for i in range(3)]).astype(bf16)
        v3[g, y, 1] = add([w1[g, 1, x]] + [v2[g, 1, i] for i in range(3)]).astype(bf16)
        ops = to("y", lambda d: (v3.at[g, y], v3.at[g, y]))
        yield
        wait(ops)
        out_ref[c, x, z, :, one] = add([v3[g, i, 0] for i in range(4)]).astype(bf16)
        out_ref[c, z, x, :, two] = add([v3[g, i, 1] for i in range(4)]).astype(bf16)
        e, f = out_ref.at[c, x, z, :, one], out_ref.at[c, z, x, :, two]
        ops = to("z", lambda d: (e, e)) + to("x", lambda d: (f, f))
        yield
        wait(ops)
        h, i = out_ref.at[c, x, :, :, one], out_ref.at[c, z, :, :, two]
        ops = to("x", lambda d: (h, h)) + to("z", lambda d: (i, i))
        yield
        wait(ops)
        k = out_ref.at[c, :, :, :, pl.ds(g * F, F)]
        ops = [sems.copy(k, k, me.sibling())]
        yield
        wait(ops)


    cts, bs, ls, ps = (ct0, ct1), (b0, b1), (l0, l1), (p0, p1)

    def rotate():
        @pl.loop(0, NB)
        def _(i):
            rows = pl.ds(pl.multiple_of(i * RB, RB), RB)
            for g in range(G):
                v = dot(x_ref[rows, :], rot_ref[:, pl.ds(g * F, F)]).astype(bf16)
                y_ref[g, rows, :] = v
                yt_ref[g, :, rows] = v.T

    def turn_x():
        @pl.loop(0, 4)
        def _(i):
            rows = pl.ds(pl.multiple_of(i * 256, 256), 256)
            xt_ref[:, rows] = x_ref[rows, :].T

    def words(g, j):
        return cb_ref[g, j // 2, pl.ds((j % 2) * 2, 2)].reshape(KC, F)

    def prepare(g):
        factor = s_ref[g] * LOG2E
        for j in range(NK):
            ks = pl.ds(j * KC, KC)
            v = words(g, j)
            cts[g % 2][:, ks] = v.T
            v32 = v.astype(f32)
            sq = jnp.sum(v32 * v32, axis=1, keepdims=True) * factor
            bs[g % 2][ks, :] = jnp.broadcast_to(sq, (KC, 128))

    def logits(g, rb, l):
        yt = yt_ref[g, :, pl.ds(rb * RB, RB)]
        scale = s_ref[g] * (2.0 * LOG2E)
        m = None
        for j in range(NK):
            ks = pl.ds(j * KC, KC)
            v = dot(words(g, j), yt) * scale - jnp.tile(bs[g % 2][ks, :], (1, RB // 128))
            l[ks, :] = v
            w = jnp.max(v.reshape(KC // 8, 8, RB), axis=0)
            m = w if m is None else jnp.maximum(m, w)
        return jnp.max(m, axis=0, keepdims=True)

    def softmax(l, m, p, cols):
        tot = None
        for j in range(NK):
            ks = pl.ds(j * KC, KC)
            e = jnp.exp2(l[ks, :] - m)
            w = jnp.sum(e.reshape(KC // 8, 8, RB), axis=0)
            tot = w if tot is None else tot + w
            p[ks, cols] = e.astype(bf16)
        inv = (1.0 / jnp.sum(tot, axis=0, keepdims=True)).astype(bf16)
        for j in range(NK):
            ks = pl.ds(j * KC, KC)
            p[ks, cols] = p[ks, cols] * inv

    def recon(g, rb, p):
        rows = pl.ds(rb * RB, RB)
        recon_ref[rows, pl.ds(g * F, F)] = dot(cts[g % 2][...], p[:, rows]).T.astype(bf16)

    def sums(g, q, p):
        n = K // NB
        pq = p[pl.ds(q * n, n), :]
        s_sum[g, q] = dot(pq, y_ref[g]).astype(bf16).reshape(4, 2, 64, F)
        t = pq[:, :128]
        for i in range(1, R // 128):
            t = t + pq[:, i * 128:(i + 1) * 128]
        ones = jnp.ones((8, 128), bf16)
        row = lax.dot_general(ones, t, (((1,), (1,)), ((), ())), preferred_element_type=f32)
        for i in range(4):
            n_ref[q, pl.ds(g * 4 + i, 1), :] = row[:1, i * 128:(i + 1) * 128]

    def cross(g):
        cols = pl.ds(g * F, F)
        u_ref[:, :, :, :, cols] = dot(xt_ref[...], recon_ref[:, cols]).astype(bf16).reshape(2, 4, 4, 32, F)


    stage_y = gather_own()
    load_x.wait()
    load_rot.wait()
    mine.wait()
    wait(stage_y)
    first = [gather_first(0)]
    rotate()
    wait(first[0])
    second = [gather_second(0)]
    first.append(gather_first(1))
    turn_x()
    wait(first[1])
    wait(second[0])
    last = [gather_core(0)]
    second.append(gather_second(1))
    first.append(gather_first(2))
    wait(last[0])
    prepare(0)

    tasks = []

    def begin(now, task, dues):
        next(task)
        tasks.append([task, now + dues[0], dues[1:]])

    def tick(now):
        for entry in list(tasks):
            task, due, dues = entry
            if now >= due:
                if next(task, task) is task:
                    tasks.remove(entry)
                else:
                    entry[1], entry[2] = now + dues[0], dues[1:]

    steps = [(g, rb) for g in range(G) for rb in range(NB)]
    m = logits(0, 0, l0)
    for t, (g, rb) in enumerate(steps):
        if g + 1 < G:
            if rb == 1:
                wait(second[g + 1])
                last.append(gather_core(g + 1))
                if g + 2 < G:
                    wait(first[g + 2])
                    second.append(gather_second(g + 2))
                if g + 3 < G:
                    first.append(gather_first(g + 3))
            if rb == 2:
                wait(last[g + 1])
                prepare(g + 1)
        nm = logits(*steps[t + 1], ls[(t + 1) % 2]) if t + 1 < len(steps) else None
        softmax(ls[t % 2], m, ps[g % 2], pl.ds(rb * RB, RB))
        if t:
            pg, pr = steps[t - 1]
            recon(pg, pr, ps[pg % 2])
        if g and g < G - 1:
            sums(g - 1, rb, ps[(g - 1) % 2])
        if g and rb == 0:
            cross(g - 1)
        tick(t)
        if g and rb == 0:
            begin(t, cross_task(g - 1), (1, 3, 2, 2, 2, 3, 1))
        if g and g < G - 1 and rb == 3:
            begin(t, sums_task(g - 1), (2, 4, 3))
        m = nm

    recon(G - 1, NB - 1, ps[(G - 1) % 2])
    cross(G - 1)
    late = 1 << 20
    chain = cross_task(G - 1)
    next(chain)
    for q in range(NB):
        sums(G - 2, q, ps[(G - 2) % 2])
    one = sums_task(G - 2)
    next(one)
    next(chain)
    tick(late)
    for q in range(NB):
        sums(G - 1, q, ps[(G - 1) % 2])
    two, count = sums_task(G - 1), counts_task()
    next(two)
    next(count)
    next(one)
    next(count)
    next(chain)
    next(two)
    for entry in tasks:
        entry[1] = 0
    tick(late)
    next(count)
    next(chain)
    next(one)
    for entry in tasks:
        entry[1] = 0
    tick(late)
    next(count, None)
    next(chain)
    next(two)
    next(one, None)
    for entry in tasks:
        entry[1] = 0
    tick(late)
    next(chain)
    next(two, None)
    owner = owner_task()
    next(owner)
    for entry in tasks:
        entry[1] = 0
    tick(late)
    next(chain)
    while tasks:
        for entry in tasks:
            entry[1] = 0
        tick(late)
    next(owner, None)
    next(chain, None)


COPIES = 3 + G * 13 + G * 13 + 10 + 6 + G * 29


def call(s, x, rot, own):
    any_place = pl.BlockSpec(memory_space=pl.ANY)
    return pl.pallas_call(
        kernel,
        out_shape=[
            pltpu.VMEM((1, 64, F), f32),
            pltpu.VMEM((R, D), bf16),
            pltpu.VMEM((2, 4, 4, 32, D), bf16),
        ],
        in_specs=[pl.BlockSpec(memory_space=pltpu.SMEM), any_place, any_place, VM],
        out_specs=[VM, VM, VM],
        scratch_shapes=[
            pltpu.VMEM((D, D), bf16), pltpu.VMEM((G, 4, 4, 2, 64, F), bf16),
            pltpu.VMEM((G, 4, 4, 2, 64, F), bf16), pltpu.VMEM((2, 4, 4, 32, D), bf16),
            pltpu.VMEM((4, 16, 128), f32),
            pltpu.VMEM((G, R, F), bf16), pltpu.VMEM((G, F, R), bf16), pltpu.VMEM((D, R), bf16),
            pltpu.VMEM((F, K), bf16), pltpu.VMEM((F, K), bf16),
            pltpu.VMEM((K, 128), f32), pltpu.VMEM((K, 128), f32),
            pltpu.VMEM((K, RB), f32), pltpu.VMEM((K, RB), f32),
            pltpu.VMEM((K, R), bf16), pltpu.VMEM((K, R), bf16),
            pltpu.VMEM((G, 4, 4, 64, F), bf16), pltpu.VMEM((G, 4, 4, 64, F), bf16),
            pltpu.VMEM((G, 2, 3, 4, 32, F), bf16), pltpu.VMEM((G, 2, 4, 32, F), bf16),
            pltpu.VMEM((G, 2, 3, 32, F), bf16), pltpu.VMEM((G, 64, F), bf16), pltpu.VMEM((3, 64, F), bf16),
            pltpu.VMEM((4, 16, 128), f32), pltpu.VMEM((3, 16, 128), f32), pltpu.VMEM((4, 16, 128), f32),
            pltpu.VMEM((3, 16, 128), f32), pltpu.VMEM((16, 128), f32), pltpu.VMEM((3, 16, 128), f32),
            pltpu.VMEM((16, 128), f32),
            pltpu.VMEM((G, 4, 4, 32, F), bf16), pltpu.VMEM((G, 4, 4, 32, F), bf16),
            pltpu.VMEM((G, 2, 3, 4, 32, 128), bf16), pltpu.VMEM((G, 2, 4, 32, 128), bf16),
            pltpu.VMEM((G, 2, 3, 32, 128), bf16), pltpu.VMEM((16, 128), bf16),
            pltpu.VMEM((G, 4, 2, 32, 128), bf16),
            pltpu.SemaphoreType.DMA((COPIES,)),
            pltpu.SemaphoreType.DMA((COPIES,)),
            pltpu.SemaphoreType.DMA((3,)),
        ],
        compiler_params=pltpu.CompilerParams(collective_id=0, has_side_effects=True, vmem_limit_bytes=58 << 20),
        name="quantizer_step",
    )(s, x, rot, own)


def finish_kernel(scale, new_in, recon_in, total_in, new_out, recon_out, cross_out, buf, sem):
    moves = [
        pltpu.make_async_copy(new_in, new_out, sem.at[0]),
        pltpu.make_async_copy(recon_in, recon_out, sem.at[1]),
    ]
    for op in moves:
        op.start()
    n = D // 4
    for i in range(4):
        rows = pl.ds(i * n, n)
        buf[rows, :] = total_in[rows, :].astype(f32) * scale
        op = pltpu.make_async_copy(buf.at[rows, :], cross_out.at[rows, :], sem.at[2 + i])
        op.start()
        moves.append(op)
    for op in moves:
        op.wait()


def finish(new, recon, total, scale):
    any_place = pl.BlockSpec(memory_space=pl.ANY)
    return pl.pallas_call(
        functools.partial(finish_kernel, scale),
        out_shape=[
            jax.ShapeDtypeStruct((1, 64, F), f32),
            jax.ShapeDtypeStruct((R, D), bf16),
            jax.ShapeDtypeStruct((D, D), f32),
        ],
        in_specs=[VM] * 3,
        out_specs=[any_place] * 3,
        scratch_shapes=[pltpu.VMEM((D, D), f32), pltpu.SemaphoreType.DMA((6,))],
        compiler_params=pltpu.CompilerParams(vmem_limit_bytes=16 << 20),
        name="write_results",
    )(new, recon, total)


def body(vector_window, orthogonal_matrix, centroid_table, sharpness_scale):
    new_codebook, recon, total = call(sharpness_scale, vector_window, orthogonal_matrix, centroid_table)
    total_rows = R * lax.axis_size("dp") * lax.axis_size("sub")
    return tuple(finish(new_codebook, recon, total.reshape(D, D), 1.0 / math.sqrt(total_rows)))


def solution(mesh):
    placed = (P(("dp", "sub"), None), P(), P("sub", "dp", None), P())
    return jax.shard_map(
        body,
        mesh=mesh,
        in_specs=placed,
        out_specs=(P("sub", "dp", None), P(("dp", "sub"), None), P()),
        check_vma=False,
    )
```

```python
import functools
import math

import jax
import jax.numpy as jnp
from jax import lax
from jax.experimental import pallas as pl
from jax.experimental.pallas import tpu as pltpu
from jax.sharding import PartitionSpec as P

LOG2E = math.log2(math.e)
G, F, K, D, R = 4, 256, 2048, 1024, 1024
RB = 256
NB = R // RB
KC = 256
NK = K // KC
f32, bf16 = jnp.float32, jnp.bfloat16
MESH = pl.DeviceIdType.MESH
VM = pl.BlockSpec(memory_space=pltpu.VMEM)


def dot(a, b):
    return jnp.dot(a, b, preferred_element_type=f32)


class Place:
    def __init__(self):
        dp, self.y = lax.axis_index("dp"), lax.axis_index("sub")
        self.x, self.z, self.c = dp // 8, (dp // 2) % 4, dp % 2

    def at(self, axis):
        return {"x": self.x, "y": self.y, "z": self.z}[axis]

    def step(self, axis, d):
        return (self.at(axis) + d) % 4

    def peer(self, axis, d):
        x, y, z = self.x, self.y, self.z
        if axis == "x":
            x = self.step("x", d)
        if axis == "y":
            y = self.step("y", d)
        if axis == "z":
            z = self.step("z", d)
        return ((x * 4 + z) * 2 + self.c, y)

    def sibling(self):
        return ((self.x * 4 + self.z) * 2 + 1 - self.c, self.y)

    def greet(self):
        barrier = pltpu.get_barrier_semaphore()
        for axis in "xyz":
            for d in (1, 2, 3):
                pl.semaphore_signal(barrier, inc=1, device_id=self.peer(axis, d), device_id_type=MESH)
        pl.semaphore_signal(barrier, inc=1, device_id=self.sibling(), device_id_type=MESH)
        pl.semaphore_wait(barrier, 10)


class Sems:
    def __init__(self, send, recv):
        self.send, self.recv, self.n = send, recv, 0

    def copy(self, src, dst, device):
        i = self.n
        self.n += 1
        op = pltpu.make_async_remote_copy(
            src_ref=src, dst_ref=dst, send_sem=self.send.at[i], recv_sem=self.recv.at[i],
            device_id=device, device_id_type=MESH,
        )
        op.start()
        return op


def wait(copies):
    for op in copies:
        op.wait()


RING = (1, 2, 3)
TOP, LOW = pl.ds(0, 32), pl.ds(32, 32)


def add(refs):
    total = refs[0].astype(f32)
    for r in refs[1:]:
        total = total + r.astype(f32)
    return total


def kernel(s_ref, x_hbm, rot_hbm, own_ref, new_ref, recon_ref, out_ref,
           rot_ref, cb_ref, s_sum, u_ref, n_ref,
           y_ref, yt_ref, xt_ref, ct0, ct1, b0, b1, l0, l1, p0, p1,
           s0, r0, r1, t1, r2, t2, r3, n0, n1, m1, n2, m2, n3, m3,
           u0, v0, v1, v2, v3, send, recv, lsem):
    me = Place()
    sems = Sems(send, recv)
    x, y, z, c = me.x, me.y, me.z, me.c

    def to(axis, pairs):
        return [sems.copy(*pairs(d), me.peer(axis, d)) for d in RING]

    x_ref = recon_ref
    load_x = pltpu.make_async_copy(x_hbm, x_ref, lsem.at[0])
    load_rot = pltpu.make_async_copy(rot_hbm, rot_ref, lsem.at[1])
    mine = pltpu.make_async_copy(own_ref.at[0], cb_ref.at[y, x, z, c], lsem.at[2])
    load_x.start()
    load_rot.start()
    mine.start()
    me.greet()


    def gather_own():
        return to("y", lambda d: (own_ref.at[0], cb_ref.at[y, x, z, c]))

    def gather_first(g):
        a, b = cb_ref.at[g, x, z, c, TOP], cb_ref.at[g, x, z, c, LOW]
        return to("x", lambda d: (a, a)) + to("z", lambda d: (b, b))

    def gather_second(g):
        a, b = cb_ref.at[g, :, z, c, TOP], cb_ref.at[g, x, :, c, LOW]
        return to("z", lambda d: (a, a)) + to("x", lambda d: (b, b))

    def gather_core(g):
        a = cb_ref.at[g, :, :, c]
        return [sems.copy(a, a, me.sibling())]

    def sums_task(g):
        ops = [sems.copy(s_sum.at[g, :, :, 1 - c], r0.at[g], me.sibling())]
        yield
        wait(ops)

        @pl.loop(0, 4)
        def _(i):
            s0[g, i] = add([s_sum[g, i, :, c], r0[g, i]]).astype(bf16)

        ops = to("x", lambda d: (s0.at[g, me.step("x", d), :, TOP], r1.at[g, 0, d - 1]))
        ops += to("z", lambda d: (s0.at[g, :, me.step("z", d), LOW], r1.at[g, 1, d - 1]))
        yield
        wait(ops)
        t1[g, 0] = add([s0[g, x, :, TOP]] + [r1[g, 0, i] for i in range(3)]).astype(bf16)
        t1[g, 1] = add([s0[g, :, z, LOW]] + [r1[g, 1, i] for i in range(3)]).astype(bf16)
        ops = to("z", lambda d: (t1.at[g, 0, me.step("z", d)], r2.at[g, 0, d - 1]))
        ops += to("x", lambda d: (t1.at[g, 1, me.step("x", d)], r2.at[g, 1, d - 1]))
        yield
        wait(ops)
        t2[g, TOP] = add([t1[g, 0, z]] + [r2[g, 0, i] for i in range(3)]).astype(bf16)
        t2[g, LOW] = add([t1[g, 1, x]] + [r2[g, 1, i] for i in range(3)]).astype(bf16)

    def counts_task():
        ops = [sems.copy(n_ref, n0, me.sibling())]
        yield
        wait(ops)
        m1[...] = n_ref[...] + n0[...]
        ops = to("x", lambda d: (m1.at[me.step("x", d)], n1.at[d - 1]))
        yield
        wait(ops)
        m2[...] = m1[x] + n1[0] + n1[1] + n1[2]
        ops = to("z", lambda d: (m2, n2.at[d - 1]))
        yield
        wait(ops)
        m3[...] = m2[...] + n2[0] + n2[1] + n2[2]

    def owner_task():
        ops = to("y", lambda d: (t2.at[me.step("y", d)], r3.at[d - 1]))
        ops += to("y", lambda d: (m3, n3.at[d - 1]))
        yield
        wait(ops)
        sums = add([t2[y]] + [r3[i] for i in range(3)])
        rows = m3[...] + n3[0] + n3[1] + n3[2]
        at_row = lax.broadcasted_iota(jnp.int32, (16, 128), 0) == y * 4 + z
        row = jnp.sum(jnp.where(at_row, rows, 0.0), axis=0, keepdims=True)
        spread = jnp.broadcast_to(row, (64, 128))
        lane, sub = lax.broadcasted_iota(jnp.int32, (64, 128), 1), lax.broadcasted_iota(jnp.int32, (64, 128), 0)
        count = jnp.sum(jnp.where(lane == sub + c * 64, spread, 0.0), axis=1, keepdims=True)
        new_ref[0] = (sums + own_ref[0].astype(f32)) / (count + 1.0)

    def cross_task(g):
        halves = [(0, ("x", "z", "y")), (1, ("z", "y", "x"))]
        lanes = (pl.ds(0, 128), pl.ds(128, 128))
        cols = (pl.ds(g * F, 128), pl.ds(g * F + 128, 128))

        def all_to(n, pairs):
            return [op for p, a in halves for op in to(a[n], functools.partial(pairs, p, a))]

        ops = [sems.copy(u_ref.at[1 - c, :, :, :, pl.ds(g * F, F)], v0.at[g], me.sibling())]
        yield
        wait(ops)
        for i in range(4):
            u0[g, i] = add([u_ref[c, i, :, :, pl.ds(g * F, F)], v0[g, i]]).astype(bf16)
        ops = all_to(0, lambda p, a, d: (u0.at[g, me.step(a[0], d), :, :, lanes[p]], v1.at[g, p, d - 1]))
        yield
        wait(ops)
        for p, a in halves:
            v2[g, p, me.at(a[1])] = add(
                [u0[g, me.at(a[0]), :, :, lanes[p]]] + [v1[g, p, i] for i in range(3)]
            ).astype(bf16)
        ops = all_to(1, lambda p, a, d: (v2.at[g, p, me.at(a[1])], v2.at[g, p, me.at(a[1])]))
        yield
        wait(ops)
        for p, a in halves:
            v3[g, p, me.at(a[2])] = add([v2[g, p, i] for i in range(4)]).astype(bf16)
        ops = all_to(2, lambda p, a, d: (v3.at[g, p, me.at(a[2])], v3.at[g, p, me.at(a[2])]))
        yield
        wait(ops)
        for p, a in halves:
            out_ref[c, me.at(a[0]), :, :, cols[p]] = add([v3[g, p, i] for i in range(4)]).astype(bf16)

        def part(p, a):
            return out_ref.at[c, me.at(a[0]), :, :, cols[p]]

        ops = all_to(0, lambda p, a, d: (part(p, a), part(p, a)))
        yield
        wait(ops)
        k = out_ref.at[c, :, :, :, pl.ds(g * F, F)]
        ops = [sems.copy(k, k, me.sibling())]
        yield
        wait(ops)


    cts, bs, ls, ps = (ct0, ct1), (b0, b1), (l0, l1), (p0, p1)

    def rotate():
        @pl.loop(0, NB)
        def _(i):
            rows = pl.ds(pl.multiple_of(i * RB, RB), RB)
            for g in range(G):
                v = dot(x_ref[rows, :], rot_ref[:, pl.ds(g * F, F)]).astype(bf16)
                y_ref[g, rows, :] = v
                yt_ref[g, :, rows] = v.T

    def turn_x():
        @pl.loop(0, 4)
        def _(i):
            rows = pl.ds(pl.multiple_of(i * 256, 256), 256)
            xt_ref[:, rows] = x_ref[rows, :].T

    def words(g, j):
        return cb_ref[g, j // 2, pl.ds((j % 2) * 2, 2)].reshape(KC, F)

    def prepare(g):
        factor = s_ref[g] * LOG2E
        for j in range(NK):
            ks = pl.ds(j * KC, KC)
            v = words(g, j)
            cts[g % 2][:, ks] = v.T
            v32 = v.astype(f32)
            sq = jnp.sum(v32 * v32, axis=1, keepdims=True) * factor
            bs[g % 2][ks, :] = jnp.broadcast_to(sq, (KC, 128))

    def logits(g, rb, l):
        yt = yt_ref[g, :, pl.ds(rb * RB, RB)]
        scale = s_ref[g] * (2.0 * LOG2E)
        m = None
        for h in range(2):
            big = dot(cb_ref[g, pl.ds(h * 2, 2)].reshape(K // 2, F), yt)
            for j in range(NK // 2):
                ks = pl.ds(h * K // 2 + j * KC, KC)
                v = big[j * KC:(j + 1) * KC] * scale - jnp.tile(bs[g % 2][ks, :], (1, RB // 128))
                l[ks, :] = v
                w = jnp.max(v.reshape(KC // 8, 8, RB), axis=0)
                m = w if m is None else jnp.maximum(m, w)
        return jnp.max(m, axis=0, keepdims=True)

    def softmax(l, m, p, cols):
        tot = None
        for j in range(NK):
            ks = pl.ds(j * KC, KC)
            e = jnp.exp2(l[ks, :] - m)
            w = jnp.sum(e.reshape(KC // 8, 8, RB), axis=0)
            tot = w if tot is None else tot + w
            p[ks, cols] = e.astype(bf16)
        inv = (1.0 / jnp.sum(tot, axis=0, keepdims=True)).astype(bf16)
        for j in range(NK):
            ks = pl.ds(j * KC, KC)
            p[ks, cols] = p[ks, cols] * inv

    def recon(g, rb, p):
        rows = pl.ds(rb * RB, RB)
        recon_ref[rows, pl.ds(g * F, F)] = dot(cts[g % 2][...], p[:, rows]).T.astype(bf16)

    def sums(g, q, p):
        n = K // NB
        pq = p[pl.ds(q * n, n), :]
        s_sum[g, q] = dot(pq, y_ref[g]).astype(bf16).reshape(4, 2, 64, F)
        t = pq[:, :128]
        for i in range(1, R // 128):
            t = t + pq[:, i * 128:(i + 1) * 128]
        row = jnp.sum(t.astype(f32).T, axis=0, keepdims=True)
        for i in range(4):
            n_ref[q, pl.ds(g * 4 + i, 1), :] = row[:, i * 128:(i + 1) * 128]

    def cross(g):
        cols = pl.ds(g * F, F)
        u_ref[:, :, :, :, cols] = dot(xt_ref[...], recon_ref[:, cols]).astype(bf16).reshape(2, 4, 4, 32, F)


    stage_y = gather_own()
    load_x.wait()
    load_rot.wait()
    mine.wait()
    wait(stage_y)
    first = [gather_first(0)]
    rotate()
    wait(first[0])
    second = [gather_second(0)]
    first.append(gather_first(1))
    turn_x()
    wait(first[1])
    wait(second[0])
    last = [gather_core(0)]
    second.append(gather_second(1))
    first.append(gather_first(2))
    wait(last[0])
    prepare(0)

    tasks = []

    def begin(now, task, dues):
        next(task)
        tasks.append([task, now + dues[0], dues[1:]])

    def tick(now):
        for entry in list(tasks):
            task, due, dues = entry
            if now >= due:
                if next(task, task) is task:
                    tasks.remove(entry)
                else:
                    entry[1], entry[2] = now + dues[0], dues[1:]

    steps = [(g, rb) for g in range(G) for rb in range(NB)]
    m = logits(0, 0, l0)
    for t, (g, rb) in enumerate(steps):
        if g and rb % 2:
            tick(t)
        if g and rb == 1:
            begin(t, cross_task(g - 1), (2, 4, 4, 4, 4, 2))
        if g and rb == 3:
            begin(t, sums_task(g - 1), (2, 4, 4))
        if g + 1 < G and rb == 1:
            wait(second[g + 1])
            last.append(gather_core(g + 1))
            if g + 2 < G:
                wait(first[g + 2])
                second.append(gather_second(g + 2))
            if g + 3 < G:
                first.append(gather_first(g + 3))
        if g + 1 < G and rb == 3:
            wait(last[g + 1])
            prepare(g + 1)
        nm = logits(*steps[t + 1], ls[(t + 1) % 2]) if t + 1 < len(steps) else None
        softmax(ls[t % 2], m, ps[g % 2], pl.ds(rb * RB, RB))
        if t:
            pg, pr = steps[t - 1]
            recon(pg, pr, ps[pg % 2])
        if g and rb < 2:
            sums(g - 1, rb * 2, ps[(g - 1) % 2])
            sums(g - 1, rb * 2 + 1, ps[(g - 1) % 2])
        if g and rb == 0:
            cross(g - 1)
        m = nm

    recon(G - 1, NB - 1, ps[(G - 1) % 2])
    cross(G - 1)
    late = 1 << 20
    chain, two, count = cross_task(G - 1), sums_task(G - 1), counts_task()
    one = tasks.pop()[0]

    def others():
        for entry in tasks:
            entry[1] = 0
        tick(late)

    next(chain)
    next(one)
    for q in range(NB):
        sums(G - 1, q, ps[(G - 1) % 2])
    next(two)
    next(count)
    next(chain)
    next(two)
    next(count)
    others()
    next(chain)
    next(one)
    next(count)
    others()
    next(chain)
    next(two)
    next(one, None)
    next(count, None)
    others()
    next(chain)
    next(two, None)
    owner = owner_task()
    next(owner)
    others()
    next(chain)
    while tasks:
        others()
    next(owner, None)
    next(chain, None)


COPIES = 3 + G * 13 + G * 13 + 10 + 6 + G * 26


def call(s, x, rot, own):
    any_place = pl.BlockSpec(memory_space=pl.ANY)
    return pl.pallas_call(
        kernel,
        out_shape=[
            pltpu.VMEM((1, 64, F), f32),
            pltpu.VMEM((R, D), bf16),
            pltpu.VMEM((2, 4, 4, 32, D), bf16),
        ],
        in_specs=[pl.BlockSpec(memory_space=pltpu.SMEM), any_place, any_place, VM],
        out_specs=[VM, VM, VM],
        scratch_shapes=[
            pltpu.VMEM((D, D), bf16), pltpu.VMEM((G, 4, 4, 2, 64, F), bf16),
            pltpu.VMEM((G, 4, 4, 2, 64, F), bf16), pltpu.VMEM((2, 4, 4, 32, D), bf16),
            pltpu.VMEM((4, 16, 128), f32),
            pltpu.VMEM((G, R, F), bf16), pltpu.VMEM((G, F, R), bf16), pltpu.VMEM((D, R), bf16),
            pltpu.VMEM((F, K), bf16), pltpu.VMEM((F, K), bf16),
            pltpu.VMEM((K, 128), f32), pltpu.VMEM((K, 128), f32),
            pltpu.VMEM((K, RB), f32), pltpu.VMEM((K, RB), f32),
            pltpu.VMEM((K, R), bf16), pltpu.VMEM((K, R), bf16),
            pltpu.VMEM((G, 4, 4, 64, F), bf16), pltpu.VMEM((G, 4, 4, 64, F), bf16),
            pltpu.VMEM((G, 2, 3, 4, 32, F), bf16), pltpu.VMEM((G, 2, 4, 32, F), bf16),
            pltpu.VMEM((G, 2, 3, 32, F), bf16), pltpu.VMEM((G, 64, F), bf16), pltpu.VMEM((3, 64, F), bf16),
            pltpu.VMEM((4, 16, 128), f32), pltpu.VMEM((3, 16, 128), f32), pltpu.VMEM((4, 16, 128), f32),
            pltpu.VMEM((3, 16, 128), f32), pltpu.VMEM((16, 128), f32), pltpu.VMEM((3, 16, 128), f32),
            pltpu.VMEM((16, 128), f32),
            pltpu.VMEM((G, 4, 4, 32, F), bf16), pltpu.VMEM((G, 4, 4, 32, F), bf16),
            pltpu.VMEM((G, 2, 3, 4, 32, 128), bf16), pltpu.VMEM((G, 2, 4, 4, 32, 128), bf16),
            pltpu.VMEM((G, 2, 4, 4, 32, 128), bf16),
            pltpu.SemaphoreType.DMA((COPIES,)),
            pltpu.SemaphoreType.DMA((COPIES,)),
            pltpu.SemaphoreType.DMA((3,)),
        ],
        compiler_params=pltpu.CompilerParams(collective_id=0, has_side_effects=True, vmem_limit_bytes=58 << 20),
        name="quantizer_step",
    )(s, x, rot, own)


def finish_kernel(scale, new_in, recon_in, total_in, new_out, recon_out, cross_out, buf, sem):
    moves = [
        pltpu.make_async_copy(new_in, new_out, sem.at[0]),
        pltpu.make_async_copy(recon_in, recon_out, sem.at[1]),
    ]
    for op in moves:
        op.start()
    n = D // 4
    for i in range(4):
        rows = pl.ds(i * n, n)
        buf[rows, :] = total_in[rows, :].astype(f32) * scale
        op = pltpu.make_async_copy(buf.at[rows, :], cross_out.at[rows, :], sem.at[2 + i])
        op.start()
        moves.append(op)
    for op in moves:
        op.wait()


def finish(new, recon, total, scale):
    any_place = pl.BlockSpec(memory_space=pl.ANY)
    return pl.pallas_call(
        functools.partial(finish_kernel, scale),
        out_shape=[
            jax.ShapeDtypeStruct((1, 64, F), f32),
            jax.ShapeDtypeStruct((R, D), bf16),
            jax.ShapeDtypeStruct((D, D), f32),
        ],
        in_specs=[VM] * 3,
        out_specs=[any_place] * 3,
        scratch_shapes=[pltpu.VMEM((D, D), f32), pltpu.SemaphoreType.DMA((6,))],
        compiler_params=pltpu.CompilerParams(vmem_limit_bytes=16 << 20),
        name="write_results",
    )(new, recon, total)


def body(vector_window, orthogonal_matrix, centroid_table, sharpness_scale):
    new_codebook, recon, total = call(sharpness_scale, vector_window, orthogonal_matrix, centroid_table)
    total_rows = R * lax.axis_size("dp") * lax.axis_size("sub")
    return tuple(finish(new_codebook, recon, total.reshape(D, D), 1.0 / math.sqrt(total_rows)))


def solution(mesh):
    placed = (P(("dp", "sub"), None), P(), P("sub", "dp", None), P())
    return jax.shard_map(
        body,
        mesh=mesh,
        in_specs=placed,
        out_specs=(P("sub", "dp", None), P(("dp", "sub"), None), P()),
        check_vma=False,
    )
```

```python
import functools
import math

import jax
import jax.numpy as jnp
from jax import lax
from jax.experimental import pallas as pl
from jax.experimental.pallas import tpu as pltpu
from jax.sharding import PartitionSpec as P

LOG2E = math.log2(math.e)
G, F, K, D, R = 4, 256, 2048, 1024, 1024
RB = 256
NB = R // RB
KC = 256
NK = K // KC
f32, bf16 = jnp.float32, jnp.bfloat16
MESH = pl.DeviceIdType.MESH
VM = pl.BlockSpec(memory_space=pltpu.VMEM)


def dot(a, b):
    return jnp.dot(a, b, preferred_element_type=f32)


class Place:
    def __init__(self):
        dp, self.y = lax.axis_index("dp"), lax.axis_index("sub")
        self.x, self.z, self.c = dp // 8, (dp // 2) % 4, dp % 2

    def at(self, axis):
        return {"x": self.x, "y": self.y, "z": self.z}[axis]

    def step(self, axis, d):
        return (self.at(axis) + d) % 4

    def peer(self, axis, d):
        x, y, z = self.x, self.y, self.z
        if axis == "x":
            x = self.step("x", d)
        if axis == "y":
            y = self.step("y", d)
        if axis == "z":
            z = self.step("z", d)
        return ((x * 4 + z) * 2 + self.c, y)

    def sibling(self):
        return ((self.x * 4 + self.z) * 2 + 1 - self.c, self.y)

    def greet(self):
        barrier = pltpu.get_barrier_semaphore()
        for axis in "xyz":
            for d in (1, 2, 3):
                pl.semaphore_signal(barrier, inc=1, device_id=self.peer(axis, d), device_id_type=MESH)
        pl.semaphore_signal(barrier, inc=1, device_id=self.sibling(), device_id_type=MESH)
        pl.semaphore_wait(barrier, 10)


class Sems:
    def __init__(self, send, recv):
        self.send, self.recv, self.n = send, recv, 0

    def copy(self, src, dst, device):
        i = self.n
        self.n += 1
        op = pltpu.make_async_remote_copy(
            src_ref=src, dst_ref=dst, send_sem=self.send.at[i], recv_sem=self.recv.at[i],
            device_id=device, device_id_type=MESH,
        )
        op.start()
        return op


def wait(copies):
    for op in copies:
        op.wait()


RING = (1, 2, 3)
TOP, LOW = pl.ds(0, 32), pl.ds(32, 32)


def add(refs):
    total = refs[0].astype(f32)
    for r in refs[1:]:
        total = total + r.astype(f32)
    return total


def kernel(s_ref, x_hbm, rot_hbm, own_ref, new_ref, recon_ref, out_ref,
           rot_ref, cb_ref, s_sum, u_ref, n_ref,
           y_ref, yt_ref, xt_ref, ct0, ct1, b0, b1, l0, l1, p0, p1,
           s0, r0, r1, t1, r2, t2, r3, n0, n1, m1, n2, m2, n3, m3,
           u0, v0, v1, v2, v3, send, recv, lsem):
    me = Place()
    sems = Sems(send, recv)
    x, y, z, c = me.x, me.y, me.z, me.c

    def to(axis, pairs):
        return [sems.copy(*pairs(d), me.peer(axis, d)) for d in RING]

    x_ref = recon_ref
    load_x = pltpu.make_async_copy(x_hbm, x_ref, lsem.at[0])
    load_rot = pltpu.make_async_copy(rot_hbm, rot_ref, lsem.at[1])
    mine = pltpu.make_async_copy(own_ref.at[0], cb_ref.at[y, x, z, c], lsem.at[2])
    load_x.start()
    load_rot.start()
    mine.start()
    me.greet()


    def gather_own():
        return to("y", lambda d: (own_ref.at[0], cb_ref.at[y, x, z, c]))

    def gather_first(g):
        a, b = cb_ref.at[g, x, z, c, TOP], cb_ref.at[g, x, z, c, LOW]
        return to("x", lambda d: (a, a)) + to("z", lambda d: (b, b))

    def gather_second(g):
        a, b = cb_ref.at[g, :, z, c, TOP], cb_ref.at[g, x, :, c, LOW]
        return to("z", lambda d: (a, a)) + to("x", lambda d: (b, b))

    def gather_core(g):
        a = cb_ref.at[g, :, :, c]
        return [sems.copy(a, a, me.sibling())]

    def sums_task(g):
        ops = []
        for h in range(2):
            half = pl.ds(h * 2, 2)
            ops.append(sems.copy(s_sum.at[g, half, :, 1 - c], r0.at[g, half], me.sibling()))
            yield
        for h in range(2):
            wait([ops[h]])
            for i in (h * 2, h * 2 + 1):
                s0[g, i] = add([s_sum[g, i, :, c], r0[g, i]]).astype(bf16)
        ops = to("x", lambda d: (s0.at[g, me.step("x", d), :, TOP], r1.at[g, 0, d - 1]))
        ops += to("z", lambda d: (s0.at[g, :, me.step("z", d), LOW], r1.at[g, 1, d - 1]))
        yield
        wait(ops)
        t1[g, 0] = add([s0[g, x, :, TOP]] + [r1[g, 0, i] for i in range(3)]).astype(bf16)
        t1[g, 1] = add([s0[g, :, z, LOW]] + [r1[g, 1, i] for i in range(3)]).astype(bf16)
        ops = to("z", lambda d: (t1.at[g, 0, me.step("z", d)], r2.at[g, 0, d - 1]))
        ops += to("x", lambda d: (t1.at[g, 1, me.step("x", d)], r2.at[g, 1, d - 1]))
        yield
        wait(ops)
        t2[g, TOP] = add([t1[g, 0, z]] + [r2[g, 0, i] for i in range(3)]).astype(bf16)
        t2[g, LOW] = add([t1[g, 1, x]] + [r2[g, 1, i] for i in range(3)]).astype(bf16)

    def counts_task():
        ops = [sems.copy(n_ref, n0, me.sibling())]
        yield
        wait(ops)
        m1[...] = n_ref[...] + n0[...]
        ops = to("x", lambda d: (m1.at[me.step("x", d)], n1.at[d - 1]))
        yield
        wait(ops)
        m2[...] = m1[x] + n1[0] + n1[1] + n1[2]
        ops = to("z", lambda d: (m2, n2.at[d - 1]))
        yield
        wait(ops)
        m3[...] = m2[...] + n2[0] + n2[1] + n2[2]

    def owner_task():
        ops = to("y", lambda d: (t2.at[me.step("y", d)], r3.at[d - 1]))
        ops += to("y", lambda d: (m3, n3.at[d - 1]))
        yield
        wait(ops)
        sums = add([t2[y]] + [r3[i] for i in range(3)])
        rows = m3[...] + n3[0] + n3[1] + n3[2]
        at_row = lax.broadcasted_iota(jnp.int32, (16, 128), 0) == y * 4 + z
        row = jnp.sum(jnp.where(at_row, rows, 0.0), axis=0, keepdims=True)
        spread = jnp.broadcast_to(row, (64, 128))
        lane, sub = lax.broadcasted_iota(jnp.int32, (64, 128), 1), lax.broadcasted_iota(jnp.int32, (64, 128), 0)
        count = jnp.sum(jnp.where(lane == sub + c * 64, spread, 0.0), axis=1, keepdims=True)
        new_ref[0] = (sums + own_ref[0].astype(f32)) / (count + 1.0)

    def cross_task(g):
        halves = [(0, ("x", "z", "y")), (1, ("z", "y", "x"))]
        lanes = (pl.ds(0, 128), pl.ds(128, 128))
        cols = (pl.ds(g * F, 128), pl.ds(g * F + 128, 128))

        def all_to(n, pairs):
            return [op for p, a in halves for op in to(a[n], functools.partial(pairs, p, a))]

        ops = [sems.copy(u_ref.at[1 - c, :, :, :, pl.ds(g * F, F)], v0.at[g], me.sibling())]
        yield
        wait(ops)
        for i in range(4):
            u0[g, i] = add([u_ref[c, i, :, :, pl.ds(g * F, F)], v0[g, i]]).astype(bf16)
        ops = all_to(0, lambda p, a, d: (u0.at[g, me.step(a[0], d), :, :, lanes[p]], v1.at[g, p, d - 1]))
        yield
        wait(ops)
        for p, a in halves:
            v2[g, p, me.at(a[1])] = add(
                [u0[g, me.at(a[0]), :, :, lanes[p]]] + [v1[g, p, i] for i in range(3)]
            ).astype(bf16)
        ops = all_to(1, lambda p, a, d: (v2.at[g, p, me.at(a[1])], v2.at[g, p, me.at(a[1])]))
        yield
        wait(ops)
        for p, a in halves:
            v3[g, p, me.at(a[2])] = add([v2[g, p, i] for i in range(4)]).astype(bf16)
        ops = all_to(2, lambda p, a, d: (v3.at[g, p, me.at(a[2])], v3.at[g, p, me.at(a[2])]))
        yield
        wait(ops)
        for p, a in halves:
            out_ref[c, me.at(a[0]), :, :, cols[p]] = add([v3[g, p, i] for i in range(4)]).astype(bf16)

        def part(p, a):
            return out_ref.at[c, me.at(a[0]), :, :, cols[p]]

        ops = all_to(0, lambda p, a, d: (part(p, a), part(p, a)))
        yield
        wait(ops)
        k = out_ref.at[c, :, :, :, pl.ds(g * F, F)]
        ops = [sems.copy(k, k, me.sibling())]
        yield
        wait(ops)


    cts, bs, ls, ps = (ct0, ct1), (b0, b1), (l0, l1), (p0, p1)

    def rotate():
        @pl.loop(0, NB)
        def _(i):
            rows = pl.ds(pl.multiple_of(i * RB, RB), RB)
            for g in range(G):
                v = dot(x_ref[rows, :], rot_ref[:, pl.ds(g * F, F)]).astype(bf16)
                y_ref[g, rows, :] = v
                yt_ref[g, :, rows] = v.T

    def turn_x():
        @pl.loop(0, 4)
        def _(i):
            rows = pl.ds(pl.multiple_of(i * 256, 256), 256)
            xt_ref[:, rows] = x_ref[rows, :].T

    def words(g, j):
        return cb_ref[g, j // 2, pl.ds((j % 2) * 2, 2)].reshape(KC, F)

    def prepare(g):
        factor = s_ref[g] * LOG2E
        for j in range(NK):
            ks = pl.ds(j * KC, KC)
            v = words(g, j)
            cts[g % 2][:, ks] = v.T
            v32 = v.astype(f32)
            sq = jnp.sum(v32 * v32, axis=1, keepdims=True) * factor
            bs[g % 2][ks, :] = jnp.broadcast_to(sq, (KC, 128))

    def logits(g, rb, l):
        yt = yt_ref[g, :, pl.ds(rb * RB, RB)]
        scale = s_ref[g] * (2.0 * LOG2E)
        m = None
        for h in range(2):
            big = dot(cb_ref[g, pl.ds(h * 2, 2)].reshape(K // 2, F), yt)
            for j in range(NK // 2):
                ks = pl.ds(h * K // 2 + j * KC, KC)
                v = big[j * KC:(j + 1) * KC] * scale - jnp.tile(bs[g % 2][ks, :], (1, RB // 128))
                l[ks, :] = v
                w = jnp.max(v.reshape(KC // 8, 8, RB), axis=0)
                m = w if m is None else jnp.maximum(m, w)
        return jnp.max(m, axis=0, keepdims=True)

    def softmax(l, m, p, cols):
        tot = None
        for j in range(NK):
            ks = pl.ds(j * KC, KC)
            e = jnp.exp2(l[ks, :] - m)
            w = jnp.sum(e.reshape(KC // 8, 8, RB), axis=0)
            tot = w if tot is None else tot + w
            p[ks, cols] = e.astype(bf16)
        inv = (1.0 / jnp.sum(tot, axis=0, keepdims=True)).astype(bf16)
        for j in range(NK):
            ks = pl.ds(j * KC, KC)
            p[ks, cols] = p[ks, cols] * inv

    def recon(g, rb, p):
        rows = pl.ds(rb * RB, RB)
        recon_ref[rows, pl.ds(g * F, F)] = dot(cts[g % 2][...], p[:, rows]).T.astype(bf16)

    def sums(g, q, p):
        n = K // NB
        pq = p[pl.ds(q * n, n), :]
        s_sum[g, q] = dot(pq, y_ref[g]).astype(bf16).reshape(4, 2, 64, F)
        t = pq[:, :128]
        for i in range(1, R // 128):
            t = t + pq[:, i * 128:(i + 1) * 128]
        row = jnp.sum(t.astype(f32).T, axis=0, keepdims=True)
        for i in range(4):
            n_ref[q, pl.ds(g * 4 + i, 1), :] = row[:, i * 128:(i + 1) * 128]

    def cross(g):
        cols = pl.ds(g * F, F)
        u_ref[:, :, :, :, cols] = dot(xt_ref[...], recon_ref[:, cols]).astype(bf16).reshape(2, 4, 4, 32, F)


    stage_y = gather_own()
    load_x.wait()
    load_rot.wait()
    mine.wait()
    wait(stage_y)
    first = [gather_first(0)]
    rotate()
    wait(first[0])
    second = [gather_second(0)]
    first.append(gather_first(1))
    turn_x()
    wait(first[1])
    wait(second[0])
    last = [gather_core(0)]
    second.append(gather_second(1))
    first.append(gather_first(2))
    wait(last[0])
    prepare(0)

    tasks = []

    def begin(now, task, dues):
        next(task)
        tasks.append([task, now + dues[0], dues[1:]])

    def tick(now):
        for entry in list(tasks):
            task, due, dues = entry
            if now >= due:
                if next(task, task) is task:
                    tasks.remove(entry)
                else:
                    entry[1], entry[2] = now + dues[0], dues[1:]

    steps = [(g, rb) for g in range(G) for rb in range(NB)]
    m = logits(0, 0, l0)
    for t, (g, rb) in enumerate(steps):
        if g and rb % 2:
            tick(t)
        if g and rb == 1:
            begin(t, cross_task(g - 1), (2, 4, 4, 4, 4, 2))
        if g and rb == 3:
            task = sums_task(g - 1)
            next(task)
            begin(t, task, (2, 4, 4))
        if g + 1 < G and rb == 1:
            wait(second[g + 1])
            last.append(gather_core(g + 1))
            if g + 2 < G:
                wait(first[g + 2])
                second.append(gather_second(g + 2))
            if g + 3 < G:
                first.append(gather_first(g + 3))
        if g + 1 < G and rb == 3:
            wait(last[g + 1])
            prepare(g + 1)
        softmax(ls[t % 2], m, ps[g % 2], pl.ds(rb * RB, RB))
        if t:
            pg, pr = steps[t - 1]
            recon(pg, pr, ps[pg % 2])
        if g and rb < 2:
            sums(g - 1, rb * 2, ps[(g - 1) % 2])
            sums(g - 1, rb * 2 + 1, ps[(g - 1) % 2])
        if g and rb == 0:
            cross(g - 1)
        nm = logits(*steps[t + 1], ls[(t + 1) % 2]) if t + 1 < len(steps) else None
        m = nm

    recon(G - 1, NB - 1, ps[(G - 1) % 2])
    cross(G - 1)
    late = 1 << 20
    chain, two, count = cross_task(G - 1), sums_task(G - 1), counts_task()
    one = tasks.pop()[0]

    def others():
        for entry in tasks:
            entry[1] = 0
        tick(late)

    next(chain)
    next(one)
    for q in range(NB):
        sums(G - 1, q, ps[(G - 1) % 2])
        if q % 2:
            next(two)
    next(count)
    next(chain)
    next(two)
    next(count)
    others()
    next(chain)
    next(one)
    next(count)
    others()
    next(chain)
    next(two)
    next(one, None)
    next(count, None)
    others()
    next(chain)
    next(two, None)
    owner = owner_task()
    next(owner)
    others()
    next(chain)
    while tasks:
        others()
    next(owner, None)
    next(chain, None)


COPIES = 3 + G * 13 + G * 14 + 10 + 6 + G * 26


def call(s, x, rot, own):
    any_place = pl.BlockSpec(memory_space=pl.ANY)
    return pl.pallas_call(
        kernel,
        out_shape=[
            pltpu.VMEM((1, 64, F), f32),
            pltpu.VMEM((R, D), bf16),
            pltpu.VMEM((2, 4, 4, 32, D), bf16),
        ],
        in_specs=[pl.BlockSpec(memory_space=pltpu.SMEM), any_place, any_place, VM],
        out_specs=[VM, VM, VM],
        scratch_shapes=[
            pltpu.VMEM((D, D), bf16), pltpu.VMEM((G, 4, 4, 2, 64, F), bf16),
            pltpu.VMEM((G, 4, 4, 2, 64, F), bf16), pltpu.VMEM((2, 4, 4, 32, D), bf16),
            pltpu.VMEM((4, 16, 128), f32),
            pltpu.VMEM((G, R, F), bf16), pltpu.VMEM((G, F, R), bf16), pltpu.VMEM((D, R), bf16),
            pltpu.VMEM((F, K), bf16), pltpu.VMEM((F, K), bf16),
            pltpu.VMEM((K, 128), f32), pltpu.VMEM((K, 128), f32),
            pltpu.VMEM((K, RB), f32), pltpu.VMEM((K, RB), f32),
            pltpu.VMEM((K, R), bf16), pltpu.VMEM((K, R), bf16),
            pltpu.VMEM((G, 4, 4, 64, F), bf16), pltpu.VMEM((G, 4, 4, 64, F), bf16),
            pltpu.VMEM((G, 2, 3, 4, 32, F), bf16), pltpu.VMEM((G, 2, 4, 32, F), bf16),
            pltpu.VMEM((G, 2, 3, 32, F), bf16), pltpu.VMEM((G, 64, F), bf16), pltpu.VMEM((3, 64, F), bf16),
            pltpu.VMEM((4, 16, 128), f32), pltpu.VMEM((3, 16, 128), f32), pltpu.VMEM((4, 16, 128), f32),
            pltpu.VMEM((3, 16, 128), f32), pltpu.VMEM((16, 128), f32), pltpu.VMEM((3, 16, 128), f32),
            pltpu.VMEM((16, 128), f32),
            pltpu.VMEM((G, 4, 4, 32, F), bf16), pltpu.VMEM((G, 4, 4, 32, F), bf16),
            pltpu.VMEM((G, 2, 3, 4, 32, 128), bf16), pltpu.VMEM((G, 2, 4, 4, 32, 128), bf16),
            pltpu.VMEM((G, 2, 4, 4, 32, 128), bf16),
            pltpu.SemaphoreType.DMA((COPIES,)),
            pltpu.SemaphoreType.DMA((COPIES,)),
            pltpu.SemaphoreType.DMA((3,)),
        ],
        compiler_params=pltpu.CompilerParams(collective_id=0, has_side_effects=True, vmem_limit_bytes=58 << 20),
        name="quantizer_step",
    )(s, x, rot, own)


def finish_kernel(scale, new_in, recon_in, total_in, new_out, recon_out, cross_out, buf, sem):
    moves = [
        pltpu.make_async_copy(new_in, new_out, sem.at[0]),
        pltpu.make_async_copy(recon_in, recon_out, sem.at[1]),
    ]
    for op in moves:
        op.start()
    n = D // 8
    for i in range(8):
        rows = pl.ds(i * n, n)
        buf[rows, :] = total_in[rows, :].astype(f32) * scale
        op = pltpu.make_async_copy(buf.at[rows, :], cross_out.at[rows, :], sem.at[2 + i])
        op.start()
        moves.append(op)
    for op in moves:
        op.wait()


def finish(new, recon, total, scale):
    any_place = pl.BlockSpec(memory_space=pl.ANY)
    return pl.pallas_call(
        functools.partial(finish_kernel, scale),
        out_shape=[
            jax.ShapeDtypeStruct((1, 64, F), f32),
            jax.ShapeDtypeStruct((R, D), bf16),
            jax.ShapeDtypeStruct((D, D), f32),
        ],
        in_specs=[VM] * 3,
        out_specs=[any_place] * 3,
        scratch_shapes=[pltpu.VMEM((D, D), f32), pltpu.SemaphoreType.DMA((10,))],
        compiler_params=pltpu.CompilerParams(vmem_limit_bytes=16 << 20),
        name="write_results",
    )(new, recon, total)


def body(vector_window, orthogonal_matrix, centroid_table, sharpness_scale):
    new_codebook, recon, total = call(sharpness_scale, vector_window, orthogonal_matrix, centroid_table)
    total_rows = R * lax.axis_size("dp") * lax.axis_size("sub")
    return tuple(finish(new_codebook, recon, total.reshape(D, D), 1.0 / math.sqrt(total_rows)))


def solution(mesh):
    placed = (P(("dp", "sub"), None), P(), P("sub", "dp", None), P())
    return jax.shard_map(
        body,
        mesh=mesh,
        in_specs=placed,
        out_specs=(P("sub", "dp", None), P(("dp", "sub"), None), P()),
        check_vma=False,
    )
```

```python
import functools
import math

import jax
import jax.numpy as jnp
from jax import lax
from jax.experimental import pallas as pl
from jax.experimental.pallas import tpu as pltpu
from jax.sharding import PartitionSpec as P

LOG2E = math.log2(math.e)
G, F, K, D, R = 4, 256, 2048, 1024, 1024
RB = 256
NB = R // RB
KC = 256
NK = K // KC
f32, bf16 = jnp.float32, jnp.bfloat16
MESH = pl.DeviceIdType.MESH
VM = pl.BlockSpec(memory_space=pltpu.VMEM)


def dot(a, b):
    return jnp.dot(a, b, preferred_element_type=f32)


class Place:
    def __init__(self):
        dp, self.y = lax.axis_index("dp"), lax.axis_index("sub")
        self.x, self.z, self.c = dp // 8, (dp // 2) % 4, dp % 2

    def at(self, axis):
        return {"x": self.x, "y": self.y, "z": self.z}[axis]

    def step(self, axis, d):
        return (self.at(axis) + d) % 4

    def peer(self, axis, d):
        x, y, z = self.x, self.y, self.z
        if axis == "x":
            x = self.step("x", d)
        if axis == "y":
            y = self.step("y", d)
        if axis == "z":
            z = self.step("z", d)
        return ((x * 4 + z) * 2 + self.c, y)

    def sibling(self):
        return ((self.x * 4 + self.z) * 2 + 1 - self.c, self.y)

    def greet(self):
        barrier = pltpu.get_barrier_semaphore()
        for axis in "xyz":
            for d in (1, 2, 3):
                pl.semaphore_signal(barrier, inc=1, device_id=self.peer(axis, d), device_id_type=MESH)
        pl.semaphore_signal(barrier, inc=1, device_id=self.sibling(), device_id_type=MESH)
        pl.semaphore_wait(barrier, 10)


class Sems:
    def __init__(self, send, recv):
        self.send, self.recv, self.n = send, recv, 0

    def copy(self, src, dst, device):
        i = self.n
        self.n += 1
        op = pltpu.make_async_remote_copy(
            src_ref=src, dst_ref=dst, send_sem=self.send.at[i], recv_sem=self.recv.at[i],
            device_id=device, device_id_type=MESH,
        )
        op.start()
        return op


def wait(copies):
    for op in copies:
        op.wait()


RING = (1, 2, 3)
TOP, LOW = pl.ds(0, 32), pl.ds(32, 32)


def add(refs):
    total = refs[0].astype(f32)
    for r in refs[1:]:
        total = total + r.astype(f32)
    return total


def kernel(s_ref, x_hbm, rot_hbm, own_ref, new_ref, recon_ref, out_ref,
           rot_ref, cb_ref, s_sum, u_ref, n_ref,
           y_ref, yt_ref, xt_ref, ct0, ct1, b0, b1, l0, l1, p0, p1,
           s0, r0, r1, t1, r2, t2, r3, n0, n1, m1, n2, m2, n3, m3,
           u0, v0, v1, v2, v3, send, recv, lsem):
    me = Place()
    sems = Sems(send, recv)
    x, y, z, c = me.x, me.y, me.z, me.c

    def to(axis, pairs):
        return [sems.copy(*pairs(d), me.peer(axis, d)) for d in RING]

    x_ref = recon_ref
    load_x = pltpu.make_async_copy(x_hbm, x_ref, lsem.at[0])
    load_rot = pltpu.make_async_copy(rot_hbm, rot_ref, lsem.at[1])
    mine = pltpu.make_async_copy(own_ref.at[0], cb_ref.at[y, x, z, c], lsem.at[2])
    load_x.start()
    load_rot.start()
    mine.start()
    me.greet()


    def gather_own():
        return to("y", lambda d: (own_ref.at[0], cb_ref.at[y, x, z, c]))

    def gather_first(g):
        a, b = cb_ref.at[g, x, z, c, TOP], cb_ref.at[g, x, z, c, LOW]
        return to("x", lambda d: (a, a)) + to("z", lambda d: (b, b))

    def gather_second(g):
        a, b = cb_ref.at[g, :, z, c, TOP], cb_ref.at[g, x, :, c, LOW]
        return to("z", lambda d: (a, a)) + to("x", lambda d: (b, b))

    def gather_core(g):
        a = cb_ref.at[g, :, :, c]
        return [sems.copy(a, a, me.sibling())]

    def sums_task(g):
        ops = []
        for h in range(2):
            half = pl.ds(h * 2, 2)
            ops.append(sems.copy(s_sum.at[g, half, :, 1 - c], r0.at[g, half], me.sibling()))
            yield
        for h in range(2):
            wait([ops[h]])
            for i in (h * 2, h * 2 + 1):
                s0[g, i] = add([s_sum[g, i, :, c], r0[g, i]]).astype(bf16)
        ops = to("x", lambda d: (s0.at[g, me.step("x", d), :, TOP], r1.at[g, 0, d - 1]))
        ops += to("z", lambda d: (s0.at[g, :, me.step("z", d), LOW], r1.at[g, 1, d - 1]))
        yield
        wait(ops)
        t1[g, 0] = add([s0[g, x, :, TOP]] + [r1[g, 0, i] for i in range(3)]).astype(bf16)
        t1[g, 1] = add([s0[g, :, z, LOW]] + [r1[g, 1, i] for i in range(3)]).astype(bf16)
        ops = to("z", lambda d: (t1.at[g, 0, me.step("z", d)], r2.at[g, 0, d - 1]))
        ops += to("x", lambda d: (t1.at[g, 1, me.step("x", d)], r2.at[g, 1, d - 1]))
        yield
        wait(ops)
        t2[g, TOP] = add([t1[g, 0, z]] + [r2[g, 0, i] for i in range(3)]).astype(bf16)
        t2[g, LOW] = add([t1[g, 1, x]] + [r2[g, 1, i] for i in range(3)]).astype(bf16)

    def counts_task():
        ops = [sems.copy(n_ref, n0, me.sibling())]
        yield
        wait(ops)
        m1[...] = n_ref[...] + n0[...]
        ops = to("x", lambda d: (m1.at[me.step("x", d)], n1.at[d - 1]))
        yield
        wait(ops)
        m2[...] = m1[x] + n1[0] + n1[1] + n1[2]
        ops = to("z", lambda d: (m2, n2.at[d - 1]))
        yield
        wait(ops)
        m3[...] = m2[...] + n2[0] + n2[1] + n2[2]

    def owner_task():
        ops = to("y", lambda d: (t2.at[me.step("y", d)], r3.at[d - 1]))
        ops += to("y", lambda d: (m3, n3.at[d - 1]))
        yield
        wait(ops)
        sums = add([t2[y]] + [r3[i] for i in range(3)])
        rows = m3[...] + n3[0] + n3[1] + n3[2]
        at_row = lax.broadcasted_iota(jnp.int32, (16, 128), 0) == y * 4 + z
        row = jnp.sum(jnp.where(at_row, rows, 0.0), axis=0, keepdims=True)
        spread = jnp.broadcast_to(row, (64, 128))
        lane, sub = lax.broadcasted_iota(jnp.int32, (64, 128), 1), lax.broadcasted_iota(jnp.int32, (64, 128), 0)
        count = jnp.sum(jnp.where(lane == sub + c * 64, spread, 0.0), axis=1, keepdims=True)
        new_ref[0] = (sums + own_ref[0].astype(f32)) / (count + 1.0)

    def cross_task(g):
        halves = [(0, ("x", "z", "y")), (1, ("z", "y", "x"))]
        lanes = (pl.ds(0, 128), pl.ds(128, 128))
        cols = (pl.ds(g * F, 128), pl.ds(g * F + 128, 128))

        def all_to(n, pairs):
            return [op for p, a in halves for op in to(a[n], functools.partial(pairs, p, a))]

        ops = [sems.copy(u_ref.at[1 - c, :, :, :, pl.ds(g * F, F)], v0.at[g], me.sibling())]
        yield
        wait(ops)
        for i in range(4):
            u0[g, i] = add([u_ref[c, i, :, :, pl.ds(g * F, F)], v0[g, i]]).astype(bf16)
        ops = all_to(0, lambda p, a, d: (u0.at[g, me.step(a[0], d), :, :, lanes[p]], v1.at[g, p, d - 1]))
        yield
        wait(ops)
        for p, a in halves:
            v2[g, p, me.at(a[1])] = add(
                [u0[g, me.at(a[0]), :, :, lanes[p]]] + [v1[g, p, i] for i in range(3)]
            ).astype(bf16)
        ops = all_to(1, lambda p, a, d: (v2.at[g, p, me.at(a[1])], v2.at[g, p, me.at(a[1])]))
        yield
        wait(ops)
        for p, a in halves:
            v3[g, p, me.at(a[2])] = add([v2[g, p, i] for i in range(4)]).astype(bf16)
        ops = all_to(2, lambda p, a, d: (v3.at[g, p, me.at(a[2])], v3.at[g, p, me.at(a[2])]))
        yield
        wait(ops)
        for p, a in halves:
            out_ref[c, me.at(a[0]), :, :, cols[p]] = add([v3[g, p, i] for i in range(4)]).astype(bf16)

        def part(p, a):
            return out_ref.at[c, me.at(a[0]), :, :, cols[p]]

        ops = all_to(0, lambda p, a, d: (part(p, a), part(p, a)))
        yield
        wait(ops)
        k = out_ref.at[c, :, :, :, pl.ds(g * F, F)]
        ops = [sems.copy(k, k, me.sibling())]
        yield
        wait(ops)


    cts, bs, ls, ps = (ct0, ct1), (b0, b1), (l0, l1), (p0, p1)

    def rotate():
        @pl.loop(0, NB)
        def _(i):
            rows = pl.ds(pl.multiple_of(i * RB, RB), RB)
            for g in range(G):
                v = dot(x_ref[rows, :], rot_ref[:, pl.ds(g * F, F)]).astype(bf16)
                y_ref[g, rows, :] = v
                yt_ref[g, :, rows] = v.T

    def turn_x():
        @pl.loop(0, 4)
        def _(i):
            rows = pl.ds(pl.multiple_of(i * 256, 256), 256)
            xt_ref[:, rows] = x_ref[rows, :].T

    def words(g, j):
        return cb_ref[g, j // 2, pl.ds((j % 2) * 2, 2)].reshape(KC, F)

    def prepare(g):
        factor = s_ref[g] * LOG2E
        for j in range(NK):
            ks = pl.ds(j * KC, KC)
            v = words(g, j)
            cts[g % 2][:, ks] = v.T
            v32 = v.astype(f32)
            sq = jnp.sum(v32 * v32, axis=1, keepdims=True) * factor
            bs[g % 2][ks, :] = jnp.broadcast_to(sq, (KC, 128))

    def logits(g, rb, l):
        yt = yt_ref[g, :, pl.ds(rb * RB, RB)]
        scale = s_ref[g] * (2.0 * LOG2E)
        m = None
        for h in range(2):
            big = dot(cb_ref[g, pl.ds(h * 2, 2)].reshape(K // 2, F), yt)
            for j in range(NK // 2):
                ks = pl.ds(h * K // 2 + j * KC, KC)
                v = big[j * KC:(j + 1) * KC] * scale - jnp.tile(bs[g % 2][ks, :], (1, RB // 128))
                l[ks, :] = v
                w = jnp.max(v.reshape(KC // 8, 8, RB), axis=0)
                m = w if m is None else jnp.maximum(m, w)
        return jnp.max(m, axis=0, keepdims=True)

    def softmax(l, m, p, cols):
        tot = None
        for j in range(NK):
            ks = pl.ds(j * KC, KC)
            e = jnp.exp2(l[ks, :] - m)
            w = jnp.sum(e.reshape(KC // 8, 8, RB), axis=0)
            tot = w if tot is None else tot + w
            p[ks, cols] = e.astype(bf16)
        inv = (1.0 / jnp.sum(tot, axis=0, keepdims=True)).astype(bf16)
        for j in range(NK):
            ks = pl.ds(j * KC, KC)
            p[ks, cols] = p[ks, cols] * inv

    def recon(g, rb, p):
        rows = pl.ds(rb * RB, RB)
        recon_ref[rows, pl.ds(g * F, F)] = dot(cts[g % 2][...], p[:, rows]).T.astype(bf16)

    def sums(g, q, p):
        n = K // NB
        pq = p[pl.ds(q * n, n), :]
        s_sum[g, q] = dot(pq, y_ref[g]).astype(bf16).reshape(4, 2, 64, F)
        t = pq[:, :128]
        for i in range(1, R // 128):
            t = t + pq[:, i * 128:(i + 1) * 128]
        row = jnp.sum(t.astype(f32).T, axis=0, keepdims=True)
        for i in range(4):
            n_ref[q, pl.ds(g * 4 + i, 1), :] = row[:, i * 128:(i + 1) * 128]

    def cross(g):
        cols = pl.ds(g * F, F)
        u_ref[:, :, :, :, cols] = dot(xt_ref[...], recon_ref[:, cols]).astype(bf16).reshape(2, 4, 4, 32, F)


    stage_y = gather_own()
    load_x.wait()
    load_rot.wait()
    mine.wait()
    wait(stage_y)
    first = [gather_first(0)]
    rotate()
    wait(first[0])
    second = [gather_second(0)]
    first.append(gather_first(1))
    turn_x()
    wait(first[1])
    wait(second[0])
    last = [gather_core(0)]
    second.append(gather_second(1))
    first.append(gather_first(2))
    wait(last[0])
    prepare(0)

    tasks = []

    def begin(now, task, dues):
        next(task)
        tasks.append([task, now + dues[0], dues[1:]])

    def tick(now):
        for entry in list(tasks):
            task, due, dues = entry
            if now >= due:
                if next(task, task) is task:
                    tasks.remove(entry)
                else:
                    entry[1], entry[2] = now + dues[0], dues[1:]

    steps = [(g, rb) for g in range(G) for rb in range(NB)]
    m = logits(0, 0, l0)
    for t, (g, rb) in enumerate(steps):
        if g and rb % 2:
            tick(t)
        if g and rb == 1:
            begin(t, cross_task(g - 1), (2, 4, 4, 4, 4, 2))
        if g and rb == 3:
            task = sums_task(g - 1)
            next(task)
            begin(t, task, (2, 4, 4))
        if g + 1 < G and rb == 1:
            wait(second[g + 1])
            last.append(gather_core(g + 1))
            if g + 2 < G:
                wait(first[g + 2])
                second.append(gather_second(g + 2))
            if g + 3 < G:
                first.append(gather_first(g + 3))
        if g + 1 < G and rb == 3:
            wait(last[g + 1])
        softmax(ls[t % 2], m, ps[g % 2], pl.ds(rb * RB, RB))
        if t:
            pg, pr = steps[t - 1]
            recon(pg, pr, ps[pg % 2])
        if g and rb < 2:
            sums(g - 1, rb * 2, ps[(g - 1) % 2])
            sums(g - 1, rb * 2 + 1, ps[(g - 1) % 2])
        if g and rb == 0:
            cross(g - 1)
        if g + 1 < G and rb == 3:
            prepare(g + 1)
        nm = logits(*steps[t + 1], ls[(t + 1) % 2]) if t + 1 < len(steps) else None
        m = nm

    recon(G - 1, NB - 1, ps[(G - 1) % 2])
    cross(G - 1)
    late = 1 << 20
    chain, two, count = cross_task(G - 1), sums_task(G - 1), counts_task()
    one = tasks.pop()[0]

    def others():
        for entry in tasks:
            entry[1] = 0
        tick(late)

    next(chain)
    next(one)
    for q in range(NB):
        sums(G - 1, q, ps[(G - 1) % 2])
        if q % 2:
            next(two)
    next(count)
    next(chain)
    next(two)
    next(count)
    others()
    next(chain)
    next(one)
    next(count)
    others()
    next(chain)
    next(two)
    next(one, None)
    next(count, None)
    others()
    next(chain)
    next(two, None)
    owner = owner_task()
    next(owner)
    others()
    next(chain)
    while tasks:
        others()
    next(owner, None)
    next(chain, None)


COPIES = 3 + G * 13 + G * 14 + 10 + 6 + G * 26


def call(s, x, rot, own):
    any_place = pl.BlockSpec(memory_space=pl.ANY)
    return pl.pallas_call(
        kernel,
        out_shape=[
            pltpu.VMEM((1, 64, F), f32),
            pltpu.VMEM((R, D), bf16),
            pltpu.VMEM((2, 4, 4, 32, D), bf16),
        ],
        in_specs=[pl.BlockSpec(memory_space=pltpu.SMEM), any_place, any_place, VM],
        out_specs=[VM, VM, VM],
        scratch_shapes=[
            pltpu.VMEM((D, D), bf16), pltpu.VMEM((G, 4, 4, 2, 64, F), bf16),
            pltpu.VMEM((G, 4, 4, 2, 64, F), bf16), pltpu.VMEM((2, 4, 4, 32, D), bf16),
            pltpu.VMEM((4, 16, 128), f32),
            pltpu.VMEM((G, R, F), bf16), pltpu.VMEM((G, F, R), bf16), pltpu.VMEM((D, R), bf16),
            pltpu.VMEM((F, K), bf16), pltpu.VMEM((F, K), bf16),
            pltpu.VMEM((K, 128), f32), pltpu.VMEM((K, 128), f32),
            pltpu.VMEM((K, RB), f32), pltpu.VMEM((K, RB), f32),
            pltpu.VMEM((K, R), bf16), pltpu.VMEM((K, R), bf16),
            pltpu.VMEM((G, 4, 4, 64, F), bf16), pltpu.VMEM((G, 4, 4, 64, F), bf16),
            pltpu.VMEM((G, 2, 3, 4, 32, F), bf16), pltpu.VMEM((G, 2, 4, 32, F), bf16),
            pltpu.VMEM((G, 2, 3, 32, F), bf16), pltpu.VMEM((G, 64, F), bf16), pltpu.VMEM((3, 64, F), bf16),
            pltpu.VMEM((4, 16, 128), f32), pltpu.VMEM((3, 16, 128), f32), pltpu.VMEM((4, 16, 128), f32),
            pltpu.VMEM((3, 16, 128), f32), pltpu.VMEM((16, 128), f32), pltpu.VMEM((3, 16, 128), f32),
            pltpu.VMEM((16, 128), f32),
            pltpu.VMEM((G, 4, 4, 32, F), bf16), pltpu.VMEM((G, 4, 4, 32, F), bf16),
            pltpu.VMEM((G, 2, 3, 4, 32, 128), bf16), pltpu.VMEM((G, 2, 4, 4, 32, 128), bf16),
            pltpu.VMEM((G, 2, 4, 4, 32, 128), bf16),
            pltpu.SemaphoreType.DMA((COPIES,)),
            pltpu.SemaphoreType.DMA((COPIES,)),
            pltpu.SemaphoreType.DMA((3,)),
        ],
        compiler_params=pltpu.CompilerParams(collective_id=0, has_side_effects=True, vmem_limit_bytes=58 << 20),
        name="quantizer_step",
    )(s, x, rot, own)


def finish_kernel(scale, new_in, recon_in, total_in, new_out, recon_out, cross_out, buf, sem):
    moves = [
        pltpu.make_async_copy(new_in, new_out, sem.at[0]),
        pltpu.make_async_copy(recon_in, recon_out, sem.at[1]),
    ]
    for op in moves:
        op.start()
    n = D // 8
    for i in range(8):
        rows = pl.ds(i * n, n)
        buf[rows, :] = total_in[rows, :].astype(f32) * scale
        op = pltpu.make_async_copy(buf.at[rows, :], cross_out.at[rows, :], sem.at[2 + i])
        op.start()
        moves.append(op)
    for op in moves:
        op.wait()


def finish(new, recon, total, scale):
    any_place = pl.BlockSpec(memory_space=pl.ANY)
    return pl.pallas_call(
        functools.partial(finish_kernel, scale),
        out_shape=[
            jax.ShapeDtypeStruct((1, 64, F), f32),
            jax.ShapeDtypeStruct((R, D), bf16),
            jax.ShapeDtypeStruct((D, D), f32),
        ],
        in_specs=[VM] * 3,
        out_specs=[any_place] * 3,
        scratch_shapes=[pltpu.VMEM((D, D), f32), pltpu.SemaphoreType.DMA((10,))],
        compiler_params=pltpu.CompilerParams(vmem_limit_bytes=16 << 20),
        name="write_results",
    )(new, recon, total)


def body(vector_window, orthogonal_matrix, centroid_table, sharpness_scale):
    new_codebook, recon, total = call(sharpness_scale, vector_window, orthogonal_matrix, centroid_table)
    total_rows = R * lax.axis_size("dp") * lax.axis_size("sub")
    return tuple(finish(new_codebook, recon, total.reshape(D, D), 1.0 / math.sqrt(total_rows)))


def solution(mesh):
    placed = (P(("dp", "sub"), None), P(), P("sub", "dp", None), P())
    return jax.shard_map(
        body,
        mesh=mesh,
        in_specs=placed,
        out_specs=(P("sub", "dp", None), P(("dp", "sub"), None), P()),
        check_vma=False,
    )
```
